32 devices in a mesh: lat: 8 (over z, y), chan: 4 (over x, core).
Axes of the slice: x: 2, y: 2, z: 4, core: 2. Of those that a mesh axis runs over, the one named last changes fastest.
Arguments:
- field: bfloat16 [32, 3, 2, 128, 4096], P('chan', None, None, 'lat'), may hold values from -6 to 6
- mix_weight: bfloat16 [32, 32], replicated, may hold values from -1 to 1
- spectral_gain: float32 [32, 2048], P('chan'), may hold values from 0.05 to 1
- legendre: bfloat16 [2, 128, 128, 1024], P(None, 'lat'), may hold values from -0.5 to 0.5
- slot_mode: int32 [128], replicated, may hold values from 0 to 127, as said below
Outputs:
- layered: bfloat16 [32, 3, 2, 128, 4096], P('chan', None, None, 'lat')
The draws below stay inside these ranges and needn't reach their ends.
Inputs may be any that keep to these rules, and one draw needn't show every extreme that they name: `slot_mode`: A permutation of the mode indices; slots 2 j and 2 j + 1 carry the modes k and 127 - k for some k, so the slots of every index of lat carry whole such pairs.
All inputs are finite; a program needn't handle non-finite values.
Results may differ from the reference program's by a relative error of at most 0.0085.
Values may be sent and summed in bfloat16 or wider, within the bound.
A program may use at most 192 MiB of HBM per device.

```python
import math
import jax
import jax.numpy as jnp
from jax import lax

CH = 32
LMAX = 2048
TAN = 3
LH = 1024
NPHI = 4096
M = 128
MSTEP = 16
NRN = 128


def draw_slot_mode(key, part):
    pair_count = M // 2
    pair_order = jax.random.permutation(jax.random.fold_in(key, 11), pair_count)
    flips = jax.random.randint(jax.random.fold_in(key, 12), (pair_count,), 0, 2)
    first_mode = jnp.where(flips == 1, pair_order, M - 1 - pair_order)
    second_mode = M - 1 - first_mode
    return jnp.stack([first_mode, second_mode], axis=1).reshape(M).astype(jnp.int32)


def level_of(key, extent, pieces, least, top_value):
    loudness = 1.0
    for dim, blocks in pieces:
        draws = jax.random.uniform(jax.random.fold_in(jax.random.fold_in(key, 6), dim), (blocks,), jnp.float32, least / len(pieces), top_value / len(pieces))
        loudness = loudness * jnp.repeat(jnp.exp(draws), extent[dim] // blocks).reshape((-1,) + (1,) * (len(extent) - 1 - dim))
    return loudness


def gaussian(own_key, extent, spread, reach, pieces=(), kind=jnp.bfloat16):
    factor_of = level_of(own_key, extent, pieces, -0.22, 0.18) if pieces else 1.0
    values = jax.random.normal(own_key, extent, jnp.float32) * spread * factor_of
    return jnp.minimum(jnp.maximum(values, -reach), reach).astype(kind)


def setup_inputs(seed: int = 0) -> dict:
    keys = jax.random.split(jax.random.key(seed), 6)
    return {
        "field": gaussian(keys[0], (CH, TAN, 2, NRN, NPHI), 1.0, 6.0, ((0, 4), (3, 8))),
        "mix_weight": gaussian(keys[1], (CH, CH), CH ** -0.5, 1.0),
        "spectral_gain": jnp.clip(jnp.exp(math.log(1.0) - 2.9957323 * jax.random.uniform(keys[2], (CH, LMAX), jnp.float32) ** level_of(keys[2], (CH, LMAX), ((0, 4),), -0.2, 0.2)), 0.05, 1.0),
        "legendre": gaussian(keys[3], (2, M, NRN, LH), NRN ** -0.5, 0.5, ((1, 8),)),
        "slot_mode": draw_slot_mode(jax.random.fold_in(keys[5], 71), 0),
    }


def reference(field, mix_weight, spectral_gain, legendre, slot_mode):
    mode_values = (slot_mode * MSTEP).astype(jnp.int32)
    places = jnp.arange(NPHI, dtype=jnp.int32)
    turns = places[:, None] * mode_values[None, :] % NPHI
    angles = turns.astype(jnp.float32) * (2.0 * math.pi / NPHI)
    basis = jnp.concatenate([jnp.cos(angles), -jnp.sin(angles)], axis=1)
    forward_table = (basis * math.sqrt(2.0 / NPHI)).astype(jnp.bfloat16)
    inverse_table = (basis.T * math.sqrt(1.0 / M)).astype(jnp.bfloat16)

    def forward(channel_block):
        rows = channel_block.reshape(-1, NPHI)
        spectra = jnp.dot(rows, forward_table, preferred_element_type=jnp.float32)
        return spectra.astype(jnp.bfloat16).reshape(TAN, 2, NRN, 2, M)
    spectrum = lax.map(forward, field)
    mixed_spec = jnp.einsum('oc,cthrqs->othrqs', mix_weight.astype(jnp.float32), spectrum.astype(jnp.float32))
    even_sum = mixed_spec[:, :, 0] + mixed_spec[:, :, 1]
    odd_sum = mixed_spec[:, :, 0] - mixed_spec[:, :, 1]
    folded = jnp.stack([even_sum, odd_sum], axis=2).astype(jnp.bfloat16)
    by_slot = jnp.moveaxis(folded, -1, 0)
    slot_tables = jnp.moveaxis(legendre, 1, 0)
    gain_par = jnp.transpose(spectral_gain.reshape(CH, LH, 2), (0, 2, 1))[:, None, :, None, :]
    degree = 2 * jnp.arange(LH, dtype=jnp.int32)[None, :] + jnp.arange(2, dtype=jnp.int32)[:, None]

    def per_slot(bundle):
        leg_table, slot_block, mode_value = bundle
        leg_table = leg_table.astype(jnp.float32)
        coefficients = jnp.einsum('ctprq,pri->ctpqi', slot_block.astype(jnp.float32), leg_table)
        allowed = (degree >= mode_value)[None, None, :, None, :]
        filtered = jnp.where(allowed, gain_par * coefficients, 0.0).astype(jnp.bfloat16)
        synthesis = jnp.einsum('ctpqi,pri->ctprq', filtered.astype(jnp.float32), leg_table)
        northern = synthesis[:, :, 0] + synthesis[:, :, 1]
        southern = synthesis[:, :, 0] - synthesis[:, :, 1]
        return jnp.stack([northern, southern], axis=2).astype(jnp.bfloat16)
    returned = lax.map(per_slot, (slot_tables, by_slot, mode_values))
    returned = jnp.moveaxis(returned, 0, -1)

    def inverse(bundle):
        spectra, initial = bundle
        rows = spectra.reshape(-1, 2 * M)
        waveform = jnp.dot(rows, inverse_table, preferred_element_type=jnp.float32).reshape(TAN, 2, NRN, NPHI)
        primal_h = waveform[0]
        sigmoid_h = jax.nn.sigmoid(primal_h)
        slope_h = sigmoid_h * (1.0 + primal_h * (1.0 - sigmoid_h))
        initial_f = initial.astype(jnp.float32)
        primal = initial_f[0] + primal_h * sigmoid_h
        tangents = initial_f[1:] + slope_h[None] * waveform[1:]
        return jnp.concatenate([primal[None], tangents], axis=0).astype(jnp.bfloat16)
    return lax.map(inverse, (returned, field))
```

```python
import functools
import math

import jax
import jax.numpy as jnp
from jax import lax
from jax.experimental import pallas as pl
from jax.experimental.pallas import tpu as pltpu
from jax.sharding import PartitionSpec as P

MESH = pl.DeviceIdType.MESH
F32 = jnp.float32
BF16 = jnp.bfloat16


def lane_iota(shape, axis):
    return lax.broadcasted_iota(jnp.int32, shape, axis)


def lane_transpose(items, width):
    count = len(items)
    group = lane_iota(items[0].shape, 1) // width
    items = list(items)
    bit = 1
    while bit < count:
        upper = (group & bit) != 0
        shift = bit * width
        lanes = items[0].shape[1]
        for first in range(count):
            if first & bit:
                continue
            low, high = items[first], items[first | bit]
            items[first] = jnp.where(upper, pltpu.roll(high, shift, 1), low)
            items[first | bit] = jnp.where(upper, high, pltpu.roll(low, lanes - shift, 1))
        bit *= 2
    return items


def phase_table(modes, shifts, period, scale):
    places = lane_iota((period, modes.shape[1]), 0)
    turns = (places * modes + shifts) & (period - 1)
    quarter = jnp.abs(turns - period // 2) - period // 4
    x = quarter.astype(F32) * (2.0 * math.pi / period)
    y = x * x
    poly = 1.0 / math.factorial(13)
    for order in (11, 9, 7, 5, 3, 1):
        sign = -1.0 if (order // 2) % 2 else 1.0
        poly = poly * y + sign / math.factorial(order)
    return x * poly * scale


def main_kernel(
    nl, nc, period, step,
    modes_ref, columns_ref, weight_ref, gain_ref, field_ref, legendre_ref, out_ref,
    field_v, legendre_v, forward_v, inverse_v, mix_v, gain_all, gain_rows,
    spec, spec_in, mixed, arranged, fold, fold_in, back, back_in, unpacked,
    field_sem, legendre_sem, gain_send, gain_recv,
    s1_send, s1_recv, s2_send, s2_recv, s3_send, s3_recv,
):
    chans, tans = field_ref.shape[0], field_ref.shape[1]
    cycles, points = field_ref.shape[3], field_ref.shape[4]
    half = legendre_ref.shape[3]
    total = nc * chans
    me_l, me_c = lax.axis_index("lat"), lax.axis_index("chan")
    everyone = nl * nc
    me = me_l * nc + me_c

    barrier = pltpu.get_barrier_semaphore()

    def greet(k, carry):
        other = lax.rem(me + k, everyone)
        pl.semaphore_signal(
            barrier, inc=1, device_id=(other // nc, lax.rem(other, nc)), device_id_type=MESH
        )
        return carry

    lax.fori_loop(1, everyone, greet, 0)

    def load_field(t):
        return pltpu.make_async_copy(field_ref.at[:, t], field_v.at[t], field_sem.at[t])

    for t in range(tans):
        load_field(t).start()
    load_legendre = pltpu.make_async_copy(
        legendre_ref.at[:, pl.ds(me_c * 4, 4)], legendre_v, legendre_sem
    )
    load_legendre.start()

    forward_v[...] = phase_table(
        columns_ref[0:1, :], columns_ref[1:2, :], period, math.sqrt(2.0 / points)
    ).astype(BF16)
    inverse_v[...] = phase_table(
        columns_ref[2:3, :], columns_ref[3:4, :], period, math.sqrt(1.0 / (period // 2))
    ).T.astype(BF16)

    rows = chans * 2 * cycles
    wide = total * 2 * cycles
    spread = (lane_iota((total, wide), 1) // (2 * cycles) == lane_iota((total, wide), 0)).astype(BF16)
    for block in range(nc):
        pick = lane_iota((rows, total), 0) // (2 * cycles) + block * chans
        pick = (pick == lane_iota((rows, total), 1)).astype(BF16)
        part = lax.dot_general(
            pick, weight_ref[...], (((1,), (1,)), ((), ())), preferred_element_type=F32
        ).astype(BF16)
        part = jnp.dot(part, spread, preferred_element_type=F32)
        at_row, at_col = lane_iota((rows, wide), 0), lane_iota((rows, wide), 1)
        part = jnp.where((at_row & at_col & cycles) != 0, -part, part)
        same = (at_row & (cycles - 1)) == (at_col & (cycles - 1))
        mix_v[block * rows:(block + 1) * rows, :] = jnp.where(same, part, 0.0).astype(BF16)

    pl.semaphore_wait(barrier, everyone - 1)

    def to_chan(source, target, send, recv):
        def one(k, carry):
            other = lax.rem(me_c + k, nc)
            pltpu.make_async_remote_copy(
                src_ref=source(other), dst_ref=target, send_sem=send, recv_sem=recv,
                device_id=(me_l, other), device_id_type=MESH,
            ).start()
            return carry
        lax.fori_loop(1, nc, one, 0)
        pltpu.make_async_copy(source(me_c), target, recv).start()

    def drain(ref, sem):
        pltpu.make_async_copy(ref, ref, sem).wait()

    to_chan(lambda other: gain_ref, gain_all.at[me_c], gain_send, gain_recv)

    def forward(t, carry):
        pltpu.make_async_copy(field_ref.at[:, t], field_v.at[t], field_sem.at[t]).wait()
        total_sum = jnp.zeros((rows, forward_v.shape[1]), F32)
        for a in range(points // period):
            x = field_v[t, :, :, :, a * period:(a + 1) * period].reshape(rows, period)
            total_sum += jnp.dot(x, forward_v[...], preferred_element_type=F32)
        spec[t] = total_sum.T.astype(BF16).reshape(spec.shape[1:])
        to_chan(lambda other: spec.at[t, other], spec_in.at[t, me_c], s1_send.at[t], s1_recv.at[t])
        return carry

    lax.fori_loop(0, tans, forward, 0)

    def mix(t, carry):
        drain(spec_in.at[t], s1_recv.at[t])
        acc = jnp.zeros(mixed.shape, F32)
        for block in range(nc):
            acc += jnp.dot(
                spec_in[t, block], mix_v[block * rows:(block + 1) * rows, :],
                preferred_element_type=F32,
            )
        mixed[...] = acc
        per_chan = 2 * chans
        for og in range(total // 4):
            items = [
                mixed[s * 2 * nl:(s + 1) * 2 * nl, og * 128:(og + 1) * 128] for s in range(4)
            ]
            for j, item in enumerate(lane_transpose(items, 2 * cycles)):
                o = og * 4 + j
                for q in range(2):
                    row = (o // chans) * per_chan + q * chans + o % chans
                    arranged[pl.ds(row, nl, stride=2 * total), :] = item[q * nl:(q + 1) * nl, :]
        fold[t] = arranged[...].astype(BF16).reshape(fold.shape[1:])

        def one(k, inner):
            other = lax.rem(me_l + k, nl)
            pltpu.make_async_remote_copy(
                src_ref=fold.at[t, other], dst_ref=fold_in.at[t, me_l],
                send_sem=s2_send.at[t], recv_sem=s2_recv.at[t],
                device_id=(other, me_c), device_id_type=MESH,
            ).start()
            return inner
        lax.fori_loop(1, nl, one, 0)
        pltpu.make_async_copy(fold.at[t, me_l], fold_in.at[t, me_l], s2_recv.at[t]).start()
        return carry

    lax.fori_loop(0, tans, mix, 0)

    load_legendre.wait()
    drain(gain_all, gain_recv)
    for p in range(2):
        pieces = []
        for block in range(nc):
            pieces += [gain_all[block, p]] * 2
        gain_rows[p] = jnp.concatenate(pieces, axis=0)

    own_slots = 4 * nc

    def legendre_stage(t, carry):
        drain(fold_in.at[t], s2_recv.at[t])
        parts = [[] for _ in range(8)]
        for lb in range(nl // 8):
            items = [fold_in[t, lb * 8 + k].astype(F32) for k in range(8)]
            for g, item in enumerate(lane_transpose(items, cycles)):
                parts[g].append(item.astype(BF16))
        degree = 2 * lane_iota((2 * total, half), 1)
        results = []
        for s in range(4):
            mode = modes_ref[me_l * own_slots + me_c * 4 + s] * step
            synthesis = []
            for p in range(2):
                source = parts[s * 2 + p]
                source = source[0] if len(source) == 1 else jnp.concatenate(source, axis=1)
                table = legendre_v[p, s]
                coefficients = jnp.dot(source, table, preferred_element_type=F32)
                filtered = jnp.where(
                    degree + p >= mode, gain_rows[p] * coefficients, 0.0
                ).astype(BF16)
                synthesis.append(lax.dot_general(
                    filtered, table, (((1,), (1,)), ((), ())), preferred_element_type=F32
                ))
            results += [synthesis[0] + synthesis[1], synthesis[0] - synthesis[1]]
        for lb in range(nl // 8):
            items = lane_transpose([r[:, lb * 128:(lb + 1) * 128] for r in results], cycles)
            for k, item in enumerate(items):
                back[t, lb * 8 + k] = item.astype(BF16).reshape(back.shape[2:])

        def one(k, inner):
            other = lax.rem(me + k, everyone)
            ol, oc = other // nc, lax.rem(other, nc)
            pltpu.make_async_remote_copy(
                src_ref=back.at[t, ol, oc], dst_ref=back_in.at[t, me_l, me_c],
                send_sem=s3_send.at[t], recv_sem=s3_recv.at[t],
                device_id=(ol, oc), device_id_type=MESH,
            ).start()
            return inner
        lax.fori_loop(1, everyone, one, 0)
        pltpu.make_async_copy(
            back.at[t, me_l, me_c], back_in.at[t, me_l, me_c], s3_recv.at[t]
        ).start()
        return carry

    lax.fori_loop(0, tans, legendre_stage, 0)

    def inverse(t, carry):
        drain(back_in.at[t], s3_recv.at[t])
        per = 2 * chans
        unpacked[...] = back_in[t].astype(F32).reshape(unpacked.shape)
        for og in range(chans // 4):
            stack = []
            for q in range(2):
                items = [
                    unpacked[pl.ds(q * chans + og * 4 + j, everyone, stride=per), :]
                    for j in range(4)
                ]
                stack += lane_transpose(items, 2 * cycles)
            left = jnp.concatenate(stack, axis=0).T.astype(BF16)
            out_ref[t, og * 128:(og + 1) * 128, :] = jnp.dot(
                left, inverse_v[...], preferred_element_type=F32
            )
        return carry

    lax.fori_loop(0, tans, inverse, 0)

    u = out_ref[0]
    g = jax.nn.sigmoid(u)
    slope = g * (1.0 + u * (1.0 - g))
    out_ref[0] = u * g
    for t in range(1, tans):
        out_ref[t] = slope * out_ref[t]

    for k in range(nc - 1):
        drain(gain_ref, gain_send)
    for t in range(tans):
        drain(spec.at[t, pl.ds(0, nc - 1)], s1_send.at[t])
        drain(fold.at[t, pl.ds(0, nl - 1)], s2_send.at[t])
        drain(back.at[t, pl.ds(0, nl - 1)], s3_send.at[t])
        drain(back.at[t, nl - 1, pl.ds(0, nc - 1)], s3_send.at[t])


def add_kernel(field_ref, delta_ref, out_ref):
    period = delta_ref.shape[2]
    points = field_ref.shape[4]
    tans, cycles = field_ref.shape[1], field_ref.shape[3]
    delta = delta_ref[...].reshape(1, tans, 2, cycles, period)
    for a in range(points // period):
        at = slice(a * period, (a + 1) * period)
        out_ref[:, :, :, :, at] = (field_ref[:, :, :, :, at].astype(F32) + delta).astype(BF16)


def local(nl, nc, field, mix_weight, spectral_gain, legendre, slot_mode):
    chans, tans, _, cycles, points = field.shape
    slots = slot_mode.shape[0]
    degrees = spectral_gain.shape[1]
    half = degrees // 2
    step = degrees // slots
    period = points // step
    full = legendre.shape[2]
    total = chans * nc
    assert slots == 4 * nc * nl and full == nl * cycles and nl % 8 == 0
    assert 2 * cycles == 32 and chans == 8 and period == 2 * slots
    ncols = 2 * slots

    by = slot_mode.reshape(nl, nc, 4)
    first = jnp.broadcast_to(jnp.transpose(by, (1, 2, 0))[:, :, None, :], (nc, 4, 2, nl))
    first_shift = jnp.broadcast_to(
        (jnp.arange(2, dtype=jnp.int32) * (period // 4))[None, None, :, None], (nc, 4, 2, nl)
    )
    second = jnp.broadcast_to(jnp.transpose(by, (2, 0, 1))[None], (2, 4, nl, nc))
    second_shift = jnp.broadcast_to(
        (jnp.arange(2, dtype=jnp.int32) * (period // 4))[:, None, None, None], (2, 4, nl, nc)
    )
    columns = jnp.stack([x.reshape(ncols) for x in (first, first_shift, second, second_shift)])
    gain = jnp.transpose(spectral_gain.reshape(chans, half, 2), (2, 0, 1))

    rows = chans * 2 * cycles
    vmem = pl.BlockSpec(memory_space=pltpu.VMEM)
    hbm = pl.BlockSpec(memory_space=pl.ANY)
    dma = pltpu.SemaphoreType.DMA
    delta = pl.pallas_call(
        functools.partial(main_kernel, nl, nc, period, step),
        out_shape=jax.ShapeDtypeStruct((tans, rows, period), F32),
        in_specs=[pl.BlockSpec(memory_space=pltpu.SMEM), vmem, vmem, vmem, hbm, hbm],
        out_specs=vmem,
        scratch_shapes=[
            pltpu.VMEM((tans, chans, 2, cycles, points), BF16),
            pltpu.VMEM((2, 4, full, half), BF16),
            pltpu.VMEM((period, ncols), BF16),
            pltpu.VMEM((ncols, period), BF16),
            pltpu.VMEM((nc * rows, total * 2 * cycles), BF16),
            pltpu.VMEM((nc, 2, chans, half), F32),
            pltpu.VMEM((2, 2 * total, half), F32),
            pltpu.VMEM((tans, nc, 8 * nl, rows), BF16),
            pltpu.VMEM((tans, nc, 8 * nl, rows), BF16),
            pltpu.VMEM((8 * nl, total * 2 * cycles), F32),
            pltpu.VMEM((nl * 2 * total, 128), F32),
            pltpu.VMEM((tans, nl, 2 * total, 128), BF16),
            pltpu.VMEM((tans, nl, 2 * total, 128), BF16),
            pltpu.VMEM((tans, nl, nc, 2 * chans, 128), BF16),
            pltpu.VMEM((tans, nl, nc, 2 * chans, 128), BF16),
            pltpu.VMEM((nl * nc * 2 * chans, 128), F32),
            dma((tans,)), dma, dma, dma,
            dma((tans,)), dma((tans,)), dma((tans,)), dma((tans,)), dma((tans,)), dma((tans,)),
        ],
        compiler_params=pltpu.CompilerParams(
            collective_id=0, has_side_effects=True, vmem_limit_bytes=56 * 1024 * 1024
        ),
        cost_estimate=pl.CostEstimate(
            flops=4_000_000_000, bytes_accessed=9_000_000, transcendentals=0
        ),
        name="spectral",
    )(slot_mode, columns, mix_weight, gain, field, legendre)

    block = (1, tans, 2, cycles, points)
    return pl.pallas_call(
        add_kernel,
        grid=(chans,),
        out_shape=jax.ShapeDtypeStruct(field.shape, BF16),
        in_specs=[
            pl.BlockSpec(block, lambda c: (c, 0, 0, 0, 0)),
            pl.BlockSpec((tans, 2 * cycles, period), lambda c: (0, c, 0)),
        ],
        out_specs=pl.BlockSpec(block, lambda c: (c, 0, 0, 0, 0)),
        compiler_params=pltpu.CompilerParams(vmem_limit_bytes=32 * 1024 * 1024),
        name="add_period",
    )(field, delta)


def solution(mesh):
    placed = (
        P("chan", None, None, "lat", None),
        P(),
        P("chan", None),
        P(None, "lat", None, None),
        P(),
    )
    return jax.shard_map(
        functools.partial(local, mesh.shape["lat"], mesh.shape["chan"]),
        mesh=mesh,
        in_specs=placed,
        out_specs=P("chan", None, None, "lat", None),
        check_vma=False,
    )
```

```python
import functools
import math

import jax
import jax.numpy as jnp
from jax import lax
from jax.experimental import pallas as pl
from jax.experimental.pallas import tpu as pltpu
from jax.sharding import PartitionSpec as P

MESH = pl.DeviceIdType.MESH
F32 = jnp.float32
BF16 = jnp.bfloat16


def lane_iota(shape, axis):
    return lax.broadcasted_iota(jnp.int32, shape, axis)


def lane_transpose(items, width):
    count = len(items)
    lane = lane_iota(items[0].shape, 1)
    items = list(items)
    bit = 1
    while bit < count:
        shift = bit * width
        upper = (lane & shift) != 0
        lanes = items[0].shape[1]
        for first in range(count):
            if first & bit:
                continue
            low, high = items[first], items[first | bit]
            items[first] = jnp.where(upper, pltpu.roll(high, shift, 1), low)
            items[first | bit] = jnp.where(upper, high, pltpu.roll(low, lanes - shift, 1))
        bit *= 2
    return items


def phase_table(modes, shifts, period, scale):
    places = lane_iota((period, modes.shape[1]), 0)
    turns = (places * modes + shifts) & (period - 1)
    quarter = jnp.abs(turns - period // 2) - period // 4
    x = quarter.astype(F32) * (2.0 * math.pi / period)
    y = x * x
    poly = 1.0 / math.factorial(13)
    for order in (11, 9, 7, 5, 3, 1):
        sign = -1.0 if (order // 2) % 2 else 1.0
        poly = poly * y + sign / math.factorial(order)
    return x * poly * scale


def bits(x, low, count):
    return lax.shift_right_logical(x, low.bit_length() - 1) & (count - 1)


def columns_of(modes, slot_of):
    slots = modes.shape[1]
    pick = (lane_iota(slot_of.shape, 0) == slot_of).astype(BF16)
    split = jnp.where(lane_iota((8, slots), 0) == 0, modes >> 4, modes & 15)
    found = jnp.dot(split.astype(F32).astype(BF16), pick, preferred_element_type=F32)
    return (found[0:1, :] * 16.0 + found[1:2, :]).astype(jnp.int32)


def main_kernel(
    nl, nc, period, step,
    modes_ref, row_ref, weight_ref, gain_ref, field_ref, legendre_ref, out_ref,
    field_v, legendre_v, forward_v, inverse_v, mix_v, gain_own, gain_all, gain_rows,
    spec, spec_in, mixed, arranged, fold, fold_in, back, back_in, unpacked, wave, slope_v,
    field_sem, out_sem, legendre_sem, gain_send, gain_recv,
    s1_send, s1_recv, s2_send, s2_recv, s3_send, s3_recv,
):
    chans, tans = field_ref.shape[0], field_ref.shape[1]
    cycles, points = field_ref.shape[3], field_ref.shape[4]
    half = legendre_ref.shape[3]
    total = nc * chans
    me_l, me_c = lax.axis_index("lat"), lax.axis_index("chan")
    everyone = nl * nc

    barrier = pltpu.get_barrier_semaphore()

    lats = [lax.rem(me_l + k, nl) for k in range(nl)]
    chs = [lax.rem(me_c + k, nc) for k in range(nc)]
    others = [(kl, kc) for kl in range(nl) for kc in range(nc) if kl or kc]
    others.sort(key=lambda pair: (-min(pair[0], nl - pair[0]), pair))
    ring = sorted(range(1, nl), key=lambda k: (-min(k, nl - k), k))

    for kl, kc in others:
        pl.semaphore_signal(
            barrier, inc=1, device_id=(lats[kl], chs[kc]), device_id_type=MESH
        )

    def load_field(t):
        return pltpu.make_async_copy(field_ref.at[:, t], field_v.at[t], field_sem.at[t])

    for t in range(tans):
        load_field(t).start()
    load_legendre = pltpu.make_async_copy(
        legendre_ref.at[:, pl.ds(me_c * 4, 4)], legendre_v, legendre_sem
    )
    load_legendre.start()

    slots = row_ref.shape[1]
    ncols = 2 * slots
    col = lane_iota((slots, ncols), 1)
    lane = lane_iota((1, ncols), 1)
    slot_of = bits(col, 1, nl) * (4 * nc) + bits(col, 8 * nl, nc) * 4 + bits(col, 2 * nl, 4)
    forward_v[...] = phase_table(
        columns_of(row_ref[...], slot_of), bits(lane, nl, 2) * (period // 4), period,
        math.sqrt(2.0 / points),
    ).astype(BF16)

    rows = chans * 2 * cycles
    wide = total * 2 * cycles
    spread = (bits(lane_iota((total, wide), 1), 2 * cycles, total) == lane_iota((total, wide), 0)).astype(BF16)
    for block in range(nc):
        pick = bits(lane_iota((rows, total), 0), 2 * cycles, chans) + block * chans
        pick = (pick == lane_iota((rows, total), 1)).astype(BF16)
        part = lax.dot_general(
            pick, weight_ref[...], (((1,), (1,)), ((), ())), preferred_element_type=F32
        ).astype(BF16)
        part = jnp.dot(part, spread, preferred_element_type=F32)
        at_row, at_col = lane_iota((rows, wide), 0), lane_iota((rows, wide), 1)
        part = jnp.where((at_row & at_col & cycles) != 0, -part, part)
        same = (at_row & (cycles - 1)) == (at_col & (cycles - 1))
        mix_v[block * rows:(block + 1) * rows, :] = jnp.where(same, part, 0.0).astype(BF16)

    pl.semaphore_wait(barrier, everyone - 1)

    def to_chan(source, target, send, recv):
        for other in chs[1:]:
            pltpu.make_async_remote_copy(
                src_ref=source(other), dst_ref=target, send_sem=send, recv_sem=recv,
                device_id=(me_l, other), device_id_type=MESH,
            ).start()
        pltpu.make_async_copy(source(me_c), target, recv).start()

    def drain(ref, sem):
        pltpu.make_async_copy(ref, ref, sem).wait()

    def forward(t, carry):
        pltpu.make_async_copy(field_ref.at[:, t], field_v.at[t], field_sem.at[t]).wait()
        total_sum = jnp.zeros((rows, forward_v.shape[1]), F32)
        for a in range(points // period):
            x = field_v[t, :, :, :, a * period:(a + 1) * period].reshape(rows, period)
            total_sum += jnp.dot(x, forward_v[...], preferred_element_type=F32)
        spec[t] = total_sum.T.astype(BF16).reshape(spec.shape[1:])
        to_chan(lambda other: spec.at[t, other], spec_in.at[t, me_c], s1_send.at[t], s1_recv.at[t])
        return carry

    lax.fori_loop(0, tans, forward, 0)

    eighth = 2 * half // 256
    x = jnp.concatenate([gain_ref[:, b * 256:(b + 1) * 256] for b in range(eighth)], axis=0)
    at_row, at_col = lane_iota((256, 256), 0), lane_iota((256, 256), 1)
    pick = (at_row == 2 * (at_col & 127) + bits(at_col, 128, 2)).astype(BF16)
    sorted_gain = jnp.zeros(x.shape, F32)
    for _ in range(3):
        term = x.astype(BF16)
        x = x - term.astype(F32)
        sorted_gain += jnp.dot(term, pick, preferred_element_type=F32)
    for b in range(eighth):
        for p in range(2):
            gain_own[p, :, b * 128:(b + 1) * 128] = (
                sorted_gain[b * chans:(b + 1) * chans, p * 128:(p + 1) * 128]
            )
    to_chan(lambda other: gain_own, gain_all.at[me_c], gain_send, gain_recv)

    slot_of = bits(col, nc, nl) * (4 * nc) + bits(col, 1, nc) * 4 + bits(col, nl * nc, 4)
    inverse_v[...] = phase_table(
        columns_of(row_ref[...], slot_of), bits(lane, slots, 2) * (period // 4), period,
        math.sqrt(1.0 / slots),
    ).T.astype(BF16)

    def mix(t, carry):
        drain(spec_in.at[t], s1_recv.at[t])
        acc = jnp.zeros(mixed.shape, F32)
        for block in range(nc):
            acc += jnp.dot(
                spec_in[t, block], mix_v[block * rows:(block + 1) * rows, :],
                preferred_element_type=F32,
            )
        mixed[...] = acc
        per_chan = 2 * chans
        for og in range(total // 4):
            items = [
                mixed[s * 2 * nl:(s + 1) * 2 * nl, og * 128:(og + 1) * 128] for s in range(4)
            ]
            for j, item in enumerate(lane_transpose(items, 2 * cycles)):
                o = og * 4 + j
                for q in range(2):
                    row = (o // chans) * per_chan + q * chans + o % chans
                    arranged[pl.ds(row, nl, stride=2 * total), :] = item[q * nl:(q + 1) * nl, :]
        fold[t] = arranged[...].astype(BF16).reshape(fold.shape[1:])

        for k in ring:
            pltpu.make_async_remote_copy(
                src_ref=fold.at[t, lats[k]], dst_ref=fold_in.at[t, me_l],
                send_sem=s2_send.at[t], recv_sem=s2_recv.at[t],
                device_id=(lats[k], me_c), device_id_type=MESH,
            ).start()
        pltpu.make_async_copy(fold.at[t, me_l], fold_in.at[t, me_l], s2_recv.at[t]).start()
        return carry

    lax.fori_loop(0, tans, mix, 0)

    load_legendre.wait()
    drain(gain_all, gain_recv)
    own_slots = 4 * nc
    degree = 2 * lane_iota((total, half), 1)
    for s in range(4):
        mode = modes_ref[me_l * own_slots + me_c * 4 + s] * step
        for p in range(2):
            gain_rows[s * 2 + p] = jnp.where(
                degree + p >= mode, gain_all[:, p].reshape(total, half), 0.0
            )

    def legendre_stage(t, carry):
        drain(fold_in.at[t], s2_recv.at[t])
        parts = [[] for _ in range(8)]
        for lb in range(nl // 8):
            items = [fold_in[t, lb * 8 + k].astype(F32) for k in range(8)]
            for g, item in enumerate(lane_transpose(items, cycles)):
                parts[g].append(item.astype(BF16))
        results = []
        for s in range(4):
            synthesis = []
            for p in range(2):
                source = parts[s * 2 + p]
                source = source[0] if len(source) == 1 else jnp.concatenate(source, axis=1)
                table = legendre_v[p, s]
                coefficients = jnp.dot(source, table, preferred_element_type=F32)
                filtered = (
                    coefficients.reshape(nc, 2, chans, half)
                    * gain_rows[s * 2 + p].reshape(nc, 1, chans, half)
                ).reshape(2 * total, half).astype(BF16)
                synthesis.append(lax.dot_general(
                    filtered, table, (((1,), (1,)), ((), ())), preferred_element_type=F32
                ))
            results += [synthesis[0] + synthesis[1], synthesis[0] - synthesis[1]]
        for lb in range(nl // 8):
            items = lane_transpose([r[:, lb * 128:(lb + 1) * 128] for r in results], cycles)
            for k, item in enumerate(items):
                back[t, lb * 8 + k] = item.astype(BF16).reshape(back.shape[2:])

        for kl, kc in others:
            pltpu.make_async_remote_copy(
                src_ref=back.at[t, lats[kl], chs[kc]], dst_ref=back_in.at[t, me_l, me_c],
                send_sem=s3_send.at[t], recv_sem=s3_recv.at[t],
                device_id=(lats[kl], chs[kc]), device_id_type=MESH,
            ).start()
        pltpu.make_async_copy(
            back.at[t, me_l, me_c], back_in.at[t, me_l, me_c], s3_recv.at[t]
        ).start()
        return carry

    lax.fori_loop(0, tans, legendre_stage, 0)

    def inverse(t):
        drain(back_in.at[t], s3_recv.at[t])
        per = 2 * chans
        unpacked[...] = back_in[t].astype(F32).reshape(unpacked.shape)
        for og in range(chans // 4):
            stack = []
            for q in range(2):
                items = [
                    unpacked[pl.ds(q * chans + og * 4 + j, everyone, stride=per), :]
                    for j in range(4)
                ]
                stack += lane_transpose(items, 2 * cycles)
            left = jnp.concatenate(stack, axis=0).T.astype(BF16)
            wave[og * 128:(og + 1) * 128, :] = jnp.dot(
                left, inverse_v[...], preferred_element_type=F32
            )

    def finish(t):
        part = wave[...].reshape(chans, 2, cycles, period)
        for a in range(points // period):
            at = slice(a * period, (a + 1) * period)
            field_v[t, :, :, :, at] = (field_v[t, :, :, :, at].astype(F32) + part).astype(BF16)
        pltpu.make_async_copy(field_v.at[t], out_ref.at[:, t], out_sem.at[t]).start()

    inverse(0)
    u = wave[...]
    g = jax.nn.sigmoid(u)
    slope_v[...] = g * (1.0 + u * (1.0 - g))
    wave[...] = u * g
    finish(0)

    def tangent(t, carry):
        inverse(t)
        wave[...] = slope_v[...] * wave[...]
        finish(t)
        return carry

    lax.fori_loop(1, tans, tangent, 0)

    for t in range(tans):
        pltpu.make_async_copy(field_v.at[t], out_ref.at[:, t], out_sem.at[t]).wait()
    for k in range(nc - 1):
        drain(gain_own, gain_send)
    for t in range(tans):
        drain(spec.at[t, pl.ds(0, nc - 1)], s1_send.at[t])
        drain(fold.at[t, pl.ds(0, nl - 1)], s2_send.at[t])
        drain(back.at[t, pl.ds(0, nl - 1)], s3_send.at[t])
        drain(back.at[t, nl - 1, pl.ds(0, nc - 1)], s3_send.at[t])


def local(nl, nc, field, mix_weight, spectral_gain, legendre, slot_mode):
    chans, tans, _, cycles, points = field.shape
    slots = slot_mode.shape[0]
    degrees = spectral_gain.shape[1]
    half = degrees // 2
    step = degrees // slots
    period = points // step
    full = legendre.shape[2]
    total = chans * nc
    assert slots == 4 * nc * nl and full == nl * cycles and nl % 8 == 0
    assert 2 * cycles == 32 and chans == 8 and period == 2 * slots
    ncols = 2 * slots

    rows = chans * 2 * cycles
    vmem = pl.BlockSpec(memory_space=pltpu.VMEM)
    hbm = pl.BlockSpec(memory_space=pl.ANY)
    dma = pltpu.SemaphoreType.DMA
    return pl.pallas_call(
        functools.partial(main_kernel, nl, nc, period, step),
        out_shape=jax.ShapeDtypeStruct(field.shape, BF16),
        in_specs=[pl.BlockSpec(memory_space=pltpu.SMEM), vmem, vmem, vmem, hbm, hbm],
        out_specs=hbm,
        scratch_shapes=[
            pltpu.VMEM((tans, chans, 2, cycles, points), BF16),
            pltpu.VMEM((2, 4, full, half), BF16),
            pltpu.VMEM((period, ncols), BF16),
            pltpu.VMEM((ncols, period), BF16),
            pltpu.VMEM((nc * rows, total * 2 * cycles), BF16),
            pltpu.VMEM((2, chans, half), F32),
            pltpu.VMEM((nc, 2, chans, half), F32),
            pltpu.VMEM((8, total, half), F32),
            pltpu.VMEM((tans, nc, 8 * nl, rows), BF16),
            pltpu.VMEM((tans, nc, 8 * nl, rows), BF16),
            pltpu.VMEM((8 * nl, total * 2 * cycles), F32),
            pltpu.VMEM((nl * 2 * total, 128), F32),
            pltpu.VMEM((tans, nl, 2 * total, 128), BF16),
            pltpu.VMEM((tans, nl, 2 * total, 128), BF16),
            pltpu.VMEM((tans, nl, nc, 2 * chans, 128), BF16),
            pltpu.VMEM((tans, nl, nc, 2 * chans, 128), BF16),
            pltpu.VMEM((nl * nc * 2 * chans, 128), F32),
            pltpu.VMEM((rows, period), F32),
            pltpu.VMEM((rows, period), F32),
            dma((tans,)), dma((tans,)), dma, dma, dma,
            dma((tans,)), dma((tans,)), dma((tans,)), dma((tans,)), dma((tans,)), dma((tans,)),
        ],
        compiler_params=pltpu.CompilerParams(
            collective_id=0, has_side_effects=True, vmem_limit_bytes=56 * 1024 * 1024
        ),
        cost_estimate=pl.CostEstimate(
            flops=4_000_000_000, bytes_accessed=9_000_000, transcendentals=0
        ),
        name="spectral",
    )(slot_mode, slot_mode.reshape(1, slots), mix_weight, spectral_gain, field, legendre)


def solution(mesh):
    placed = (
        P("chan", None, None, "lat", None),
        P(),
        P("chan", None),
        P(None, "lat", None, None),
        P(),
    )
    return jax.shard_map(
        functools.partial(local, mesh.shape["lat"], mesh.shape["chan"]),
        mesh=mesh,
        in_specs=placed,
        out_specs=P("chan", None, None, "lat", None),
        check_vma=False,
    )
```

```python
import functools
import math

import jax
import jax.numpy as jnp
from jax import lax
from jax.experimental import pallas as pl
from jax.experimental.pallas import tpu as pltpu
from jax.sharding import PartitionSpec as P

MESH = pl.DeviceIdType.MESH
F32 = jnp.float32
BF16 = jnp.bfloat16


def lane_iota(shape, axis):
    return lax.broadcasted_iota(jnp.int32, shape, axis)


def lane_transpose(items, width):
    count = len(items)
    lane = lane_iota(items[0].shape, 1)
    items = list(items)
    bit = 1
    while bit < count:
        shift = bit * width
        upper = (lane & shift) != 0
        lanes = items[0].shape[1]
        for first in range(count):
            if first & bit:
                continue
            low, high = items[first], items[first | bit]
            items[first] = jnp.where(upper, pltpu.roll(high, shift, 1), low)
            items[first | bit] = jnp.where(upper, high, pltpu.roll(low, lanes - shift, 1))
        bit *= 2
    return items


def phase_table(modes, shifts, period, scale):
    places = lane_iota((period, modes.shape[1]), 0)
    turns = (places * modes + shifts) & (period - 1)
    quarter = jnp.abs(turns - period // 2) - period // 4
    x = quarter.astype(F32) * (2.0 * math.pi / period)
    y = x * x
    poly = 1.0 / math.factorial(13)
    for order in (11, 9, 7, 5, 3, 1):
        sign = -1.0 if (order // 2) % 2 else 1.0
        poly = poly * y + sign / math.factorial(order)
    return x * poly * scale


def bits(x, low, count):
    return lax.shift_right_logical(x, low.bit_length() - 1) & (count - 1)


def columns_of(modes, slot_of):
    slots = modes.shape[1]
    pick = (lane_iota(slot_of.shape, 0) == slot_of).astype(BF16)
    split = jnp.where(lane_iota((8, slots), 0) == 0, modes >> 4, modes & 15)
    found = jnp.dot(split.astype(F32).astype(BF16), pick, preferred_element_type=F32)
    return (found[0:1, :] * 16.0 + found[1:2, :]).astype(jnp.int32)


def main_kernel(
    nl, nc, period, step,
    modes_ref, row_ref, weight_ref, gain_ref, field_ref, legendre_ref, out_ref,
    field_v, legendre_v, forward_v, inverse_v, mix_v, gain_own, gain_all, gain_rows,
    spec, spec_in, arranged, back, back_in, unpacked, wave, slope_v, row_v, weight_v, gain_v,
    field_sem, out_sem, legendre_sem, small_sem, gain_send, gain_recv,
    s1_send, s1_recv, s3_send, s3_recv,
):
    chans, tans = field_ref.shape[0], field_ref.shape[1]
    cycles, points = field_ref.shape[3], field_ref.shape[4]
    half = legendre_ref.shape[3]
    total = nc * chans
    rows = chans * 2 * cycles
    me_l, me_c = lax.axis_index("lat"), lax.axis_index("chan")
    everyone = nl * nc

    barrier = pltpu.get_barrier_semaphore()

    lats = [lax.rem(me_l + k, nl) for k in range(nl)]
    chs = [lax.rem(me_c + k, nc) for k in range(nc)]
    others = [(kl, kc) for kl in range(nl) for kc in range(nc) if kl or kc]
    others.sort(key=lambda pair: (-min(pair[0], nl - pair[0]), pair))

    for kl, kc in others:
        pl.semaphore_signal(
            barrier, inc=1, device_id=(lats[kl], chs[kc]), device_id_type=MESH
        )

    def load_field(t):
        return pltpu.make_async_copy(field_ref.at[:, t], field_v.at[t], field_sem.at[t])

    small = [
        pltpu.make_async_copy(source, target, small_sem.at[k])
        for k, (source, target) in enumerate(
            ((row_ref, row_v), (weight_ref, weight_v), (gain_ref, gain_v))
        )
    ]
    small[0].start()
    load_field(0).start()
    small[1].start()
    small[2].start()
    for t in range(1, tans):
        load_field(t).start()
    load_legendre = pltpu.make_async_copy(
        legendre_ref.at[:, pl.ds(me_c * 4, 4)], legendre_v, legendre_sem
    )
    load_legendre.start()

    small[0].wait()
    slots = row_ref.shape[1]
    ncols = 2 * slots
    col = lane_iota((slots, ncols), 1)
    lane = lane_iota((1, ncols), 1)
    forward_v[...] = phase_table(
        columns_of(row_v[...], col >> 1), (lane & 1) * (period // 4), period,
        math.sqrt(2.0 / points),
    ).astype(BF16)

    slot_of = bits(col, nc, nl) * (4 * nc) + bits(col, 1, nc) * 4 + bits(col, nl * nc, 4)
    inverse_v[...] = phase_table(
        columns_of(row_v[...], slot_of), bits(lane, slots, 2) * (period // 4), period,
        math.sqrt(1.0 / slots),
    ).T.astype(BF16)

    pl.semaphore_wait(barrier, everyone - 1)

    def to_chan(source, target, send, recv):
        for other in chs[1:]:
            pltpu.make_async_remote_copy(
                src_ref=source(other), dst_ref=target, send_sem=send, recv_sem=recv,
                device_id=(me_l, other), device_id_type=MESH,
            ).start()
        pltpu.make_async_copy(source(me_c), target, recv).start()

    def to_all(source, target, send, recv):
        for kl, kc in others:
            pltpu.make_async_remote_copy(
                src_ref=source.at[lats[kl], chs[kc]], dst_ref=target.at[me_l, me_c],
                send_sem=send, recv_sem=recv,
                device_id=(lats[kl], chs[kc]), device_id_type=MESH,
            ).start()
        pltpu.make_async_copy(source.at[me_l, me_c], target.at[me_l, me_c], recv).start()

    def drain(ref, sem):
        pltpu.make_async_copy(ref, ref, sem).wait()

    def forward(t, carry):
        pltpu.make_async_copy(field_ref.at[:, t], field_v.at[t], field_sem.at[t]).wait()
        total_sum = jnp.zeros((rows, forward_v.shape[1]), F32)
        for a in range(points // period):
            x = field_v[t, :, :, :, a * period:(a + 1) * period].reshape(rows, period)
            total_sum += jnp.dot(x, forward_v[...], preferred_element_type=F32)
        turned = total_sum.T.reshape(everyone, 8, rows)
        turned = jnp.concatenate([turned[:, :, :128], turned[:, :, 128:]], axis=1)
        spec[t] = turned.astype(BF16).reshape(spec.shape[1:])
        to_all(spec.at[t], spec_in.at[t], s1_send.at[t], s1_recv.at[t])
        return carry

    lax.fori_loop(0, tans, forward, 0)

    small[2].wait()
    eighth = 2 * half // 256
    x = jnp.concatenate([gain_v[:, b * 256:(b + 1) * 256] for b in range(eighth)], axis=0)
    at_row, at_col = lane_iota((256, 256), 0), lane_iota((256, 256), 1)
    pick = (at_row == 2 * (at_col & 127) + bits(at_col, 128, 2)).astype(BF16)
    sorted_gain = jnp.zeros(x.shape, F32)
    for _ in range(3):
        term = x.astype(BF16)
        x = x - term.astype(F32)
        sorted_gain += jnp.dot(term, pick, preferred_element_type=F32)
    for b in range(eighth):
        for p in range(2):
            gain_own[p, :, b * 128:(b + 1) * 128] = (
                sorted_gain[b * chans:(b + 1) * chans, p * 128:(p + 1) * 128]
            )
    to_chan(lambda other: gain_own, gain_all.at[me_c], gain_send, gain_recv)

    small[1].wait()
    wide = total * 2 * cycles
    spread = (bits(lane_iota((total, wide), 1), 2 * cycles, total) == lane_iota((total, wide), 0)).astype(BF16)
    for block in range(nc):
        pick = bits(lane_iota((rows, total), 0), 2 * cycles, chans) + block * chans
        pick = (pick == lane_iota((rows, total), 1)).astype(BF16)
        part = lax.dot_general(
            pick, weight_v[...], (((1,), (1,)), ((), ())), preferred_element_type=F32
        ).astype(BF16)
        part = jnp.dot(part, spread, preferred_element_type=F32)
        at_row, at_col = lane_iota((rows, wide), 0), lane_iota((rows, wide), 1)
        part = jnp.where((at_row & at_col & cycles) != 0, -part, part)
        same = (at_row & (cycles - 1)) == (at_col & (cycles - 1))
        mix_v[block * rows:(block + 1) * rows, :] = jnp.where(same, part, 0.0).astype(BF16)

    load_legendre.wait()
    drain(gain_all, gain_recv)
    own_slots = 4 * nc
    degree = 2 * lane_iota((total, half), 1)
    for s in range(4):
        mode = modes_ref[me_l * own_slots + me_c * 4 + s] * step
        for p in range(2):
            gain_rows[s * 2 + p] = jnp.where(
                degree + p >= mode, gain_all[:, p].reshape(total, half), 0.0
            )

    def legendre_stage(t, carry):
        drain(spec_in.at[t], s1_recv.at[t])
        x = spec_in[t].astype(F32)
        x = jnp.concatenate([
            x[:, block, part * 8:(part + 1) * 8, :].reshape(nl * 8, 128)
            for block in range(nc) for part in range(2)
        ], axis=1).astype(BF16)
        mixed = jnp.dot(x, mix_v[...], preferred_element_type=F32)
        for lb in range(nl // 8):
            for og in range(total // 4):
                items = [
                    mixed[l * 8:(l + 1) * 8, og * 128:(og + 1) * 128]
                    for l in range(lb * 8, lb * 8 + 8)
                ]
                for k, item in enumerate(lane_transpose(items, cycles)):
                    row = (k % 2) * 8 * total + og * 4 + k // 2
                    arranged.at[lb][pl.ds(row, 8, stride=total), :] = item
        results = []
        for s in range(4):
            synthesis = []
            for p in range(2):
                first = (p * 4 + s) * 2 * total
                source = [
                    arranged[lb, first:first + 2 * total, :].astype(BF16) for lb in range(nl // 8)
                ]
                source = source[0] if len(source) == 1 else jnp.concatenate(source, axis=1)
                table = legendre_v[p, s]
                coefficients = jnp.dot(source, table, preferred_element_type=F32)
                filtered = (
                    coefficients.reshape(2, total, half) * gain_rows[s * 2 + p][None]
                ).reshape(2 * total, half).astype(BF16)
                synthesis.append(lax.dot_general(
                    filtered, table, (((1,), (1,)), ((), ())), preferred_element_type=F32
                ))
            results += [synthesis[0] + synthesis[1], synthesis[0] - synthesis[1]]
        for lb in range(nl // 8):
            items = lane_transpose([r[:, lb * 128:(lb + 1) * 128] for r in results], cycles)
            for k, item in enumerate(items):
                item = item.reshape(2, nc, chans, 128)
                item = jnp.concatenate([item[0], item[1]], axis=1)
                back[t, lb * 8 + k] = item.astype(BF16)

        to_all(back.at[t], back_in.at[t], s3_send.at[t], s3_recv.at[t])
        return carry

    lax.fori_loop(0, tans, legendre_stage, 0)

    def inverse(t):
        drain(back_in.at[t], s3_recv.at[t])
        per = 2 * chans
        unpacked[...] = back_in[t].astype(F32).reshape(unpacked.shape)
        for og in range(chans // 4):
            stack = []
            for q in range(2):
                items = [
                    unpacked[pl.ds(q * chans + og * 4 + j, everyone, stride=per), :]
                    for j in range(4)
                ]
                stack += lane_transpose(items, 2 * cycles)
            left = jnp.concatenate(stack, axis=0).T.astype(BF16)
            wave[og * 128:(og + 1) * 128, :] = jnp.dot(
                left, inverse_v[...], preferred_element_type=F32
            )

    def finish(t):
        part = wave[...].reshape(chans, 2, cycles, period)
        for a in range(points // period):
            at = slice(a * period, (a + 1) * period)
            field_v[t, :, :, :, at] = (field_v[t, :, :, :, at].astype(F32) + part).astype(BF16)
        pltpu.make_async_copy(field_v.at[t], out_ref.at[:, t], out_sem.at[t]).start()

    inverse(0)
    u = wave[...]
    g = jax.nn.sigmoid(u)
    slope_v[...] = g * (1.0 + u * (1.0 - g))
    wave[...] = u * g
    finish(0)

    def tangent(t, carry):
        inverse(t)
        wave[...] = slope_v[...] * wave[...]
        finish(t)
        return carry

    lax.fori_loop(1, tans, tangent, 0)

    for t in range(tans):
        pltpu.make_async_copy(field_v.at[t], out_ref.at[:, t], out_sem.at[t]).wait()
    for k in range(nc - 1):
        drain(gain_own, gain_send)
    for t in range(tans):
        drain(spec.at[t, pl.ds(0, nl - 1)], s1_send.at[t])
        drain(spec.at[t, nl - 1, pl.ds(0, nc - 1)], s1_send.at[t])
        drain(back.at[t, pl.ds(0, nl - 1)], s3_send.at[t])
        drain(back.at[t, nl - 1, pl.ds(0, nc - 1)], s3_send.at[t])


def local(nl, nc, field, mix_weight, spectral_gain, legendre, slot_mode):
    chans, tans, _, cycles, points = field.shape
    slots = slot_mode.shape[0]
    degrees = spectral_gain.shape[1]
    half = degrees // 2
    step = degrees // slots
    period = points // step
    full = legendre.shape[2]
    total = chans * nc
    assert slots == 4 * nc * nl and full == nl * cycles and nl % 8 == 0
    assert 2 * cycles == 32 and chans == 8 and period == 2 * slots
    ncols = 2 * slots

    rows = chans * 2 * cycles
    hbm = pl.BlockSpec(memory_space=pltpu.HBM)
    dma = pltpu.SemaphoreType.DMA
    return pl.pallas_call(
        functools.partial(main_kernel, nl, nc, period, step),
        out_shape=jax.ShapeDtypeStruct(field.shape, BF16),
        in_specs=[pl.BlockSpec(memory_space=pltpu.SMEM)] + [hbm] * 5,
        out_specs=pl.BlockSpec(memory_space=pl.ANY),
        scratch_shapes=[
            pltpu.VMEM((tans, chans, 2, cycles, points), BF16),
            pltpu.VMEM((2, 4, full, half), BF16),
            pltpu.VMEM((period, ncols), BF16),
            pltpu.VMEM((ncols, period), BF16),
            pltpu.VMEM((nc * rows, total * 2 * cycles), BF16),
            pltpu.VMEM((2, chans, half), F32),
            pltpu.VMEM((nc, 2, chans, half), F32),
            pltpu.VMEM((8, total, half), F32),
            pltpu.VMEM((tans, nl, nc, 16, 128), BF16),
            pltpu.VMEM((tans, nl, nc, 16, 128), BF16),
            pltpu.VMEM((full // 128, 16 * total, 128), F32),
            pltpu.VMEM((tans, nl, nc, 2 * chans, 128), BF16),
            pltpu.VMEM((tans, nl, nc, 2 * chans, 128), BF16),
            pltpu.VMEM((nl * nc * 2 * chans, 128), F32),
            pltpu.VMEM((rows, period), F32),
            pltpu.VMEM((rows, period), F32),
            pltpu.VMEM((1, slots), jnp.int32),
            pltpu.VMEM((total, total), BF16),
            pltpu.VMEM((chans, degrees), F32),
            dma((tans,)), dma((tans,)), dma, dma((3,)), dma, dma,
            dma((tans,)), dma((tans,)), dma((tans,)), dma((tans,)),
        ],
        compiler_params=pltpu.CompilerParams(
            collective_id=0, has_side_effects=True, vmem_limit_bytes=44 * 1024 * 1024
        ),
        cost_estimate=pl.CostEstimate(
            flops=4_000_000_000, bytes_accessed=9_000_000, transcendentals=0
        ),
        name="spectral",
    )(slot_mode, slot_mode.reshape(1, slots), mix_weight, spectral_gain, field, legendre)


def solution(mesh):
    placed = (
        P("chan", None, None, "lat", None),
        P(),
        P("chan", None),
        P(None, "lat", None, None),
        P(),
    )
    return jax.shard_map(
        functools.partial(local, mesh.shape["lat"], mesh.shape["chan"]),
        mesh=mesh,
        in_specs=placed,
        out_specs=P("chan", None, None, "lat", None),
        check_vma=False,
    )
```

```python
import functools
import math

import jax
import jax.numpy as jnp
from jax import lax
from jax.experimental import pallas as pl
from jax.experimental.pallas import tpu as pltpu
from jax.sharding import PartitionSpec as P

MESH = pl.DeviceIdType.MESH
F32 = jnp.float32
BF16 = jnp.bfloat16


def lane_iota(shape, axis):
    return lax.broadcasted_iota(jnp.int32, shape, axis)


def lane_transpose(items, width):
    count = len(items)
    lane = lane_iota(items[0].shape, 1)
    items = list(items)
    bit = 1
    while bit < count:
        shift = bit * width
        upper = (lane & shift) != 0
        lanes = items[0].shape[1]
        for first in range(count):
            if first & bit:
                continue
            low, high = items[first], items[first | bit]
            items[first] = jnp.where(upper, pltpu.roll(high, shift, 1), low)
            items[first | bit] = jnp.where(upper, high, pltpu.roll(low, lanes - shift, 1))
        bit *= 2
    return items


def phase_table(modes, shifts, period, scale):
    places = lane_iota((period, modes.shape[1]), 0)
    turns = (places * modes + shifts) & (period - 1)
    quarter = jnp.abs(turns - period // 2) - period // 4
    x = quarter.astype(F32) * (2.0 * math.pi / period)
    y = x * x
    poly = 1.0 / math.factorial(13)
    for order in (11, 9, 7, 5, 3, 1):
        sign = -1.0 if (order // 2) % 2 else 1.0
        poly = poly * y + sign / math.factorial(order)
    return x * poly * scale


def bits(x, low, count):
    return lax.shift_right_logical(x, low.bit_length() - 1) & (count - 1)


def columns_of(modes, slot_of):
    slots = modes.shape[1]
    pick = (lane_iota(slot_of.shape, 0) == slot_of).astype(BF16)
    split = jnp.where(lane_iota((8, slots), 0) == 0, modes >> 4, modes & 15)
    found = jnp.dot(split.astype(F32).astype(BF16), pick, preferred_element_type=F32)
    return (found[0:1, :] * 16.0 + found[1:2, :]).astype(jnp.int32)


def main_kernel(
    nl, nc, period, step,
    modes_ref, row_ref, weight_ref, gain_ref, field_ref, legendre_ref, out_ref,
    field_v, legendre_v, forward_v, inverse_v, mix_v, gain_own, gain_all, gain_rows,
    spec, spec_in, arranged, back, back_in, unpacked, wave, slope_v, row_v, weight_v, gain_v,
    field_sem, out_sem, legendre_sem, small_sem, gain_send, gain_recv,
    s1_send, s1_recv, s3_send, s3_recv,
):
    chans, tans = field_ref.shape[0], field_ref.shape[1]
    cycles, points = field_ref.shape[3], field_ref.shape[4]
    half = legendre_ref.shape[3]
    total = nc * chans
    rows = chans * 2 * cycles
    me_l, me_c = lax.axis_index("lat"), lax.axis_index("chan")
    everyone = nl * nc

    barrier = pltpu.get_barrier_semaphore()

    lats = [lax.rem(me_l + k, nl) for k in range(nl)]
    chs = [lax.rem(me_c + k, nc) for k in range(nc)]
    others = [(kl, kc) for kl in range(nl) for kc in range(nc) if kl or kc]
    others.sort(key=lambda pair: (-min(pair[0], nl - pair[0]), pair))

    for kl, kc in others:
        pl.semaphore_signal(
            barrier, inc=1, device_id=(lats[kl], chs[kc]), device_id_type=MESH
        )

    def load_field(t):
        return pltpu.make_async_copy(field_ref.at[:, t], field_v.at[t], field_sem.at[t])

    small = [
        pltpu.make_async_copy(source, target, small_sem.at[k])
        for k, (source, target) in enumerate(
            ((row_ref, row_v), (weight_ref, weight_v), (gain_ref, gain_v))
        )
    ]
    small[0].start()
    load_field(0).start()
    small[1].start()
    small[2].start()
    for t in range(1, tans):
        load_field(t).start()
    load_legendre = pltpu.make_async_copy(
        legendre_ref.at[:, pl.ds(me_c * 4, 4)], legendre_v, legendre_sem
    )
    load_legendre.start()

    small[0].wait()
    slots = row_ref.shape[1]
    ncols = 2 * slots
    col = lane_iota((slots, ncols), 1)
    lane = lane_iota((1, ncols), 1)
    forward_v[...] = phase_table(
        columns_of(row_v[...], col >> 1), (lane & 1) * (period // 4), period,
        math.sqrt(2.0 / points),
    ).astype(BF16)

    slot_of = bits(col, nc, nl) * (4 * nc) + bits(col, 1, nc) * 4 + bits(col, nl * nc, 4)
    inverse_v[...] = phase_table(
        columns_of(row_v[...], slot_of), bits(lane, slots, 2) * (period // 4), period,
        math.sqrt(1.0 / slots),
    ).T.astype(BF16)

    pl.semaphore_wait(barrier, everyone - 1)

    def to_chan(source, target, send, recv):
        for other in chs[1:]:
            pltpu.make_async_remote_copy(
                src_ref=source(other), dst_ref=target, send_sem=send, recv_sem=recv,
                device_id=(me_l, other), device_id_type=MESH,
            ).start()
        pltpu.make_async_copy(source(me_c), target, recv).start()

    def to_all(source, target, send, recv):
        for kl, kc in others:
            pltpu.make_async_remote_copy(
                src_ref=source.at[lats[kl], chs[kc]], dst_ref=target.at[me_l, me_c],
                send_sem=send, recv_sem=recv,
                device_id=(lats[kl], chs[kc]), device_id_type=MESH,
            ).start()
        pltpu.make_async_copy(source.at[me_l, me_c], target.at[me_l, me_c], recv).start()

    def drain(ref, sem):
        pltpu.make_async_copy(ref, ref, sem).wait()

    def forward(t, carry):
        pltpu.make_async_copy(field_ref.at[:, t], field_v.at[t], field_sem.at[t]).wait()
        total_sum = jnp.zeros((rows, forward_v.shape[1]), F32)
        for a in range(points // period):
            x = field_v[t, :, :, :, a * period:(a + 1) * period].reshape(rows, period)
            total_sum += jnp.dot(x, forward_v[...], preferred_element_type=F32)
        turned = total_sum.T.reshape(everyone, 8, rows)
        turned = jnp.concatenate([turned[:, :, :128], turned[:, :, 128:]], axis=1)
        spec[t] = turned.astype(BF16).reshape(spec.shape[1:])
        to_all(spec.at[t], spec_in.at[t], s1_send.at[t], s1_recv.at[t])
        return carry

    lax.fori_loop(0, tans, forward, 0)

    small[2].wait()
    eighth = 2 * half // 256
    x = jnp.concatenate([gain_v[:, b * 256:(b + 1) * 256] for b in range(eighth)], axis=0)
    at_row, at_col = lane_iota((256, 256), 0), lane_iota((256, 256), 1)
    pick = (at_row == 2 * (at_col & 127) + bits(at_col, 128, 2)).astype(BF16)
    sorted_gain = jnp.zeros(x.shape, F32)
    for _ in range(3):
        term = x.astype(BF16)
        x = x - term.astype(F32)
        sorted_gain += jnp.dot(term, pick, preferred_element_type=F32)
    for b in range(eighth):
        for p in range(2):
            gain_own[p, :, b * 128:(b + 1) * 128] = (
                sorted_gain[b * chans:(b + 1) * chans, p * 128:(p + 1) * 128]
            )
    to_chan(lambda other: gain_own, gain_all.at[me_c], gain_send, gain_recv)

    small[1].wait()
    pick = ((lane_iota((2 * total, total), 0) & (total - 1)) == lane_iota((2 * total, total), 1))
    spread = (lane_iota((total, 2 * total), 1) >> 1 == lane_iota((total, 2 * total), 0))
    part = jnp.dot(pick.astype(BF16), weight_v[...], preferred_element_type=F32).astype(BF16)
    part = jnp.dot(part, spread.astype(BF16), preferred_element_type=F32)
    shape = (2 * total, 2 * total)
    both = (lane_iota(shape, 0) >= total) & ((lane_iota(shape, 1) & 1) == 1)
    mix_v[...] = jnp.where(both, -part, part).astype(BF16)

    load_legendre.wait()
    drain(gain_all, gain_recv)
    own_slots = 4 * nc
    degree = 2 * lane_iota((total, half), 1)
    for s in range(4):
        mode = modes_ref[me_l * own_slots + me_c * 4 + s] * step
        for p in range(2):
            gain_rows[s * 2 + p] = jnp.where(
                degree + p >= mode, gain_all[:, p].reshape(total, half), 0.0
            )

    def legendre_stage(t, carry):
        drain(spec_in.at[t], s1_recv.at[t])
        x = spec_in[t].astype(F32)
        mixed = []
        for lb in range(nl // 8):
            for block in range(nc):
                for part in range(2):
                    items = [
                        x[lb * 8 + k, block, part * 8:(part + 1) * 8, :] for k in range(8)
                    ]
                    for k, item in enumerate(lane_transpose(items, cycles)):
                        row = (block * 2 + part) * 8 + k
                        arranged.at[lb][pl.ds(row, 8, stride=2 * total), :] = item
            wide = jnp.concatenate([
                arranged[lb, j * 2 * total:(j + 1) * 2 * total, :] for j in range(8)
            ], axis=1).astype(BF16)
            mixed.append(jnp.dot(mix_v[...], wide, preferred_element_type=F32).astype(BF16))
        results = []
        for s in range(4):
            synthesis = []
            for p in range(2):
                source = jnp.concatenate([
                    jnp.concatenate([
                        m[p * total:(p + 1) * total, (s * 2 + q) * 128:(s * 2 + q + 1) * 128]
                        for m in mixed
                    ], axis=1) if len(mixed) > 1 else
                    mixed[0][p * total:(p + 1) * total, (s * 2 + q) * 128:(s * 2 + q + 1) * 128]
                    for q in range(2)
                ], axis=0)
                table = legendre_v[p, s]
                coefficients = jnp.dot(source, table, preferred_element_type=F32)
                filtered = (
                    coefficients.reshape(2, total, half) * gain_rows[s * 2 + p][None]
                ).reshape(2 * total, half).astype(BF16)
                synthesis.append(lax.dot_general(
                    filtered, table, (((1,), (1,)), ((), ())), preferred_element_type=F32
                ))
            results += [synthesis[0] + synthesis[1], synthesis[0] - synthesis[1]]
        for lb in range(nl // 8):
            items = lane_transpose([r[:, lb * 128:(lb + 1) * 128] for r in results], cycles)
            for k, item in enumerate(items):
                item = item.reshape(2, nc, chans, 128)
                item = jnp.concatenate([item[0], item[1]], axis=1)
                back[t, lb * 8 + k] = item.astype(BF16)

        to_all(back.at[t], back_in.at[t], s3_send.at[t], s3_recv.at[t])
        return carry

    lax.fori_loop(0, tans, legendre_stage, 0)

    def inverse(t):
        drain(back_in.at[t], s3_recv.at[t])
        per = 2 * chans
        unpacked[...] = back_in[t].astype(F32).reshape(unpacked.shape)
        for og in range(chans // 4):
            stack = []
            for q in range(2):
                items = [
                    unpacked[pl.ds(q * chans + og * 4 + j, everyone, stride=per), :]
                    for j in range(4)
                ]
                stack += lane_transpose(items, 2 * cycles)
            left = jnp.concatenate(stack, axis=0).T.astype(BF16)
            wave[og * 128:(og + 1) * 128, :] = jnp.dot(
                left, inverse_v[...], preferred_element_type=F32
            )

    def finish(t):
        part = wave[...].reshape(chans, 2, cycles, period)
        for a in range(points // period):
            at = slice(a * period, (a + 1) * period)
            field_v[t, :, :, :, at] = (field_v[t, :, :, :, at].astype(F32) + part).astype(BF16)
        pltpu.make_async_copy(field_v.at[t], out_ref.at[:, t], out_sem.at[t]).start()

    inverse(0)
    u = wave[...]
    g = jax.nn.sigmoid(u)
    slope_v[...] = g * (1.0 + u * (1.0 - g))
    wave[...] = u * g
    finish(0)

    def tangent(t, carry):
        inverse(t)
        wave[...] = slope_v[...] * wave[...]
        finish(t)
        return carry

    lax.fori_loop(1, tans, tangent, 0)

    for t in range(tans):
        pltpu.make_async_copy(field_v.at[t], out_ref.at[:, t], out_sem.at[t]).wait()
    for k in range(nc - 1):
        drain(gain_own, gain_send)
    for t in range(tans):
        drain(spec.at[t, pl.ds(0, nl - 1)], s1_send.at[t])
        drain(spec.at[t, nl - 1, pl.ds(0, nc - 1)], s1_send.at[t])
        drain(back.at[t, pl.ds(0, nl - 1)], s3_send.at[t])
        drain(back.at[t, nl - 1, pl.ds(0, nc - 1)], s3_send.at[t])


def local(nl, nc, field, mix_weight, spectral_gain, legendre, slot_mode):
    chans, tans, _, cycles, points = field.shape
    slots = slot_mode.shape[0]
    degrees = spectral_gain.shape[1]
    half = degrees // 2
    step = degrees // slots
    period = points // step
    full = legendre.shape[2]
    total = chans * nc
    assert slots == 4 * nc * nl and full == nl * cycles and nl % 8 == 0
    assert 2 * cycles == 32 and chans == 8 and period == 2 * slots
    ncols = 2 * slots

    rows = chans * 2 * cycles
    hbm = pl.BlockSpec(memory_space=pltpu.HBM)
    dma = pltpu.SemaphoreType.DMA
    return pl.pallas_call(
        functools.partial(main_kernel, nl, nc, period, step),
        out_shape=jax.ShapeDtypeStruct(field.shape, BF16),
        in_specs=[pl.BlockSpec(memory_space=pltpu.SMEM)] + [hbm] * 5,
        out_specs=pl.BlockSpec(memory_space=pl.ANY),
        scratch_shapes=[
            pltpu.VMEM((tans, chans, 2, cycles, points), BF16),
            pltpu.VMEM((2, 4, full, half), BF16),
            pltpu.VMEM((period, ncols), BF16),
            pltpu.VMEM((ncols, period), BF16),
            pltpu.VMEM((2 * total, 2 * total), BF16),
            pltpu.VMEM((2, chans, half), F32),
            pltpu.VMEM((nc, 2, chans, half), F32),
            pltpu.VMEM((8, total, half), F32),
            pltpu.VMEM((tans, nl, nc, 16, 128), BF16),
            pltpu.VMEM((tans, nl, nc, 16, 128), BF16),
            pltpu.VMEM((full // 128, 16 * total, 128), F32),
            pltpu.VMEM((tans, nl, nc, 2 * chans, 128), BF16),
            pltpu.VMEM((tans, nl, nc, 2 * chans, 128), BF16),
            pltpu.VMEM((nl * nc * 2 * chans, 128), F32),
            pltpu.VMEM((rows, period), F32),
            pltpu.VMEM((rows, period), F32),
            pltpu.VMEM((1, slots), jnp.int32),
            pltpu.VMEM((total, total), BF16),
            pltpu.VMEM((chans, degrees), F32),
            dma((tans,)), dma((tans,)), dma, dma((3,)), dma, dma,
            dma((tans,)), dma((tans,)), dma((tans,)), dma((tans,)),
        ],
        compiler_params=pltpu.CompilerParams(
            collective_id=0, has_side_effects=True, vmem_limit_bytes=44 * 1024 * 1024
        ),
        cost_estimate=pl.CostEstimate(
            flops=4_000_000_000, bytes_accessed=9_000_000, transcendentals=0
        ),
        name="spectral",
    )(slot_mode, slot_mode.reshape(1, slots), mix_weight, spectral_gain, field, legendre)


def solution(mesh):
    placed = (
        P("chan", None, None, "lat", None),
        P(),
        P("chan", None),
        P(None, "lat", None, None),
        P(),
    )
    return jax.shard_map(
        functools.partial(local, mesh.shape["lat"], mesh.shape["chan"]),
        mesh=mesh,
        in_specs=placed,
        out_specs=P("chan", None, None, "lat", None),
        check_vma=False,
    )
```

```python
import functools
import math

import jax
import jax.numpy as jnp
from jax import lax
from jax.experimental import pallas as pl
from jax.experimental.pallas import tpu as pltpu
from jax.sharding import PartitionSpec as P

MESH = pl.DeviceIdType.MESH
F32 = jnp.float32
BF16 = jnp.bfloat16


def lane_iota(shape, axis):
    return lax.broadcasted_iota(jnp.int32, shape, axis)


def lane_transpose(items, width):
    count = len(items)
    lane = lane_iota(items[0].shape, 1)
    items = list(items)
    bit = 1
    while bit < count:
        shift = bit * width
        upper = (lane & shift) != 0
        lanes = items[0].shape[1]
        for first in range(count):
            if first & bit:
                continue
            low, high = items[first], items[first | bit]
            items[first] = jnp.where(upper, pltpu.roll(high, shift, 1), low)
            items[first | bit] = jnp.where(upper, high, pltpu.roll(low, lanes - shift, 1))
        bit *= 2
    return items


def phase_table(modes, shifts, period, scale):
    places = lane_iota((period, modes.shape[1]), 0)
    turns = (places * modes + shifts) & (period - 1)
    quarter = jnp.abs(turns - period // 2) - period // 4
    x = quarter.astype(F32) * (2.0 * math.pi / period)
    y = x * x
    poly = 1.0 / math.factorial(13)
    for order in (11, 9, 7, 5, 3, 1):
        sign = -1.0 if (order // 2) % 2 else 1.0
        poly = poly * y + sign / math.factorial(order)
    return x * poly * scale


def bits(x, low, count):
    return lax.shift_right_logical(x, low.bit_length() - 1) & (count - 1)


def columns_of(modes, slot_of):
    slots = modes.shape[1]
    pick = (lane_iota(slot_of.shape, 0) == slot_of).astype(BF16)
    split = jnp.where(lane_iota((8, slots), 0) == 0, modes >> 4, modes & 15)
    found = jnp.dot(split.astype(F32).astype(BF16), pick, preferred_element_type=F32)
    return (found[0:1, :] * 16.0 + found[1:2, :]).astype(jnp.int32)


def main_kernel(
    nl, nc, slots, period, step,
    small_ref, field_ref, legendre_ref, out_ref,
    field_v, legendre_v, forward_v, inverse_v, mix_v, gain_own, gain_all, gain_rows,
    spec, spec_in, arranged, back, back_in, unpacked, wave, slope_v, small_v,
    field_sem, out_sem, legendre_sem, small_sem, gain_send, gain_recv,
    s1_send, s1_recv, s3_send, s3_recv,
):
    chans, tans = field_ref.shape[0], field_ref.shape[1]
    cycles, points = field_ref.shape[3], field_ref.shape[4]
    half = legendre_ref.shape[3]
    total = nc * chans
    rows = chans * 2 * cycles
    me_l, me_c = lax.axis_index("lat"), lax.axis_index("chan")
    everyone = nl * nc

    barrier = pltpu.get_barrier_semaphore()

    lats = [lax.rem(me_l + k, nl) for k in range(nl)]
    chs = [lax.rem(me_c + k, nc) for k in range(nc)]
    others = [(kl, kc) for kl in range(nl) for kc in range(nc) if kl or kc]
    others.sort(key=lambda pair: (-min(pair[0], nl - pair[0]), pair))

    def load_field(t):
        return pltpu.make_async_copy(field_ref.at[:, t], field_v.at[t], field_sem.at[t])

    load_small = pltpu.make_async_copy(small_ref, small_v, small_sem)
    load_small.start()
    load_field(0).start()
    for kl, kc in others:
        pl.semaphore_signal(
            barrier, inc=1, device_id=(lats[kl], chs[kc]), device_id_type=MESH
        )

    load_small.wait()
    mode_row = small_v[chans + total:chans + total + 1, :slots].astype(jnp.int32)
    ncols = 2 * slots
    col = lane_iota((slots, ncols), 1)
    lane = lane_iota((1, ncols), 1)
    forward_v[...] = phase_table(
        columns_of(mode_row, col >> 1), (lane & 1) * (period // 4), period,
        math.sqrt(2.0 / points),
    ).astype(BF16)

    pl.semaphore_wait(barrier, everyone - 1)

    def to_chan(source, target, send, recv):
        for other in chs[1:]:
            pltpu.make_async_remote_copy(
                src_ref=source(other), dst_ref=target, send_sem=send, recv_sem=recv,
                device_id=(me_l, other), device_id_type=MESH,
            ).start()
        pltpu.make_async_copy(source(me_c), target, recv).start()

    def to_all(source, target, send, recv):
        for kl, kc in others:
            pltpu.make_async_remote_copy(
                src_ref=source.at[lats[kl], chs[kc]], dst_ref=target.at[me_l, me_c],
                send_sem=send, recv_sem=recv,
                device_id=(lats[kl], chs[kc]), device_id_type=MESH,
            ).start()
        pltpu.make_async_copy(source.at[me_l, me_c], target.at[me_l, me_c], recv).start()

    def drain(ref, sem):
        pltpu.make_async_copy(ref, ref, sem).wait()

    def forward(t):
        total_sum = jnp.zeros((rows, forward_v.shape[1]), F32)
        for a in range(points // period):
            x = field_v[t, :, :, :, a * period:(a + 1) * period].reshape(rows, period)
            total_sum += jnp.dot(x, forward_v[...], preferred_element_type=F32)
        turned = total_sum.T.reshape(everyone, 8, rows)
        turned = jnp.concatenate([turned[:, :, :128], turned[:, :, 128:]], axis=1)
        spec[t] = turned.astype(BF16).reshape(spec.shape[1:])
        to_all(spec.at[t], spec_in.at[t], s1_send.at[t], s1_recv.at[t])

    load_field(0).wait()
    for t in range(1, tans):
        load_field(t).start()
    forward(0)
    load_legendre = pltpu.make_async_copy(
        legendre_ref.at[:, pl.ds(me_c * 4, 4)], legendre_v, legendre_sem
    )
    load_legendre.start()

    def forward_next(t, carry):
        pltpu.make_async_copy(field_ref.at[:, t], field_v.at[t], field_sem.at[t]).wait()
        forward(t)
        return carry

    lax.fori_loop(1, tans, forward_next, 0)

    slot_of = bits(col, nc, nl) * (4 * nc) + bits(col, 1, nc) * 4 + bits(col, nl * nc, 4)
    inverse_v[...] = phase_table(
        columns_of(mode_row, slot_of), bits(lane, slots, 2) * (period // 4), period,
        math.sqrt(1.0 / slots),
    ).T.astype(BF16)

    eighth = 2 * half // 256
    x = jnp.concatenate([small_v[:chans, b * 256:(b + 1) * 256] for b in range(eighth)], axis=0)
    at_row, at_col = lane_iota((256, 256), 0), lane_iota((256, 256), 1)
    pick = (at_row == 2 * (at_col & 127) + bits(at_col, 128, 2)).astype(BF16)
    sorted_gain = jnp.zeros(x.shape, F32)
    for _ in range(3):
        term = x.astype(BF16)
        x = x - term.astype(F32)
        sorted_gain += jnp.dot(term, pick, preferred_element_type=F32)
    for b in range(eighth):
        for p in range(2):
            gain_own[p, :, b * 128:(b + 1) * 128] = (
                sorted_gain[b * chans:(b + 1) * chans, p * 128:(p + 1) * 128]
            )
    to_chan(lambda other: gain_own, gain_all.at[me_c], gain_send, gain_recv)

    weight = small_v[chans:chans + total, :total].astype(BF16)
    pick = ((lane_iota((2 * total, total), 0) & (total - 1)) == lane_iota((2 * total, total), 1))
    spread = (lane_iota((total, 2 * total), 1) >> 1 == lane_iota((total, 2 * total), 0))
    part = jnp.dot(pick.astype(BF16), weight, preferred_element_type=F32).astype(BF16)
    part = jnp.dot(part, spread.astype(BF16), preferred_element_type=F32)
    shape = (2 * total, 2 * total)
    both = (lane_iota(shape, 0) >= total) & ((lane_iota(shape, 1) & 1) == 1)
    mix_v[...] = jnp.where(both, -part, part).astype(BF16)

    load_legendre.wait()
    drain(gain_all, gain_recv)
    own_slots = 4 * nc
    degree = 2 * lane_iota((total, half), 1)
    for s in range(4):
        here = lane_iota((1, slots), 1) == me_l * own_slots + me_c * 4 + s
        mode = jnp.sum(jnp.where(here, small_v[chans + total:chans + total + 1, :slots], 0.0))
        mode = mode.astype(jnp.int32) * step
        for p in range(2):
            gain_rows[s * 2 + p] = jnp.where(
                degree + p >= mode, gain_all[:, p].reshape(total, half), 0.0
            )

    def legendre_stage(t, carry):
        drain(spec_in.at[t], s1_recv.at[t])
        x = spec_in[t].astype(F32)
        mixed = []
        for lb in range(nl // 8):
            for block in range(nc):
                for part in range(2):
                    items = [
                        x[lb * 8 + k, block, part * 8:(part + 1) * 8, :] for k in range(8)
                    ]
                    for k, item in enumerate(lane_transpose(items, cycles)):
                        row = (block * 2 + part) * 8 + k
                        arranged.at[lb][pl.ds(row, 8, stride=2 * total), :] = item
            wide = jnp.concatenate([
                arranged[lb, j * 2 * total:(j + 1) * 2 * total, :] for j in range(8)
            ], axis=1).astype(BF16)
            mixed.append(jnp.dot(mix_v[...], wide, preferred_element_type=F32).astype(BF16))
        results = []
        for s in range(4):
            synthesis = []
            for p in range(2):
                source = jnp.concatenate([
                    jnp.concatenate([
                        m[p * total:(p + 1) * total, (s * 2 + q) * 128:(s * 2 + q + 1) * 128]
                        for m in mixed
                    ], axis=1) if len(mixed) > 1 else
                    mixed[0][p * total:(p + 1) * total, (s * 2 + q) * 128:(s * 2 + q + 1) * 128]
                    for q in range(2)
                ], axis=0)
                table = legendre_v[p, s]
                coefficients = jnp.dot(source, table, preferred_element_type=F32)
                filtered = (
                    coefficients.reshape(2, total, half) * gain_rows[s * 2 + p][None]
                ).reshape(2 * total, half).astype(BF16)
                synthesis.append(lax.dot_general(
                    filtered, table, (((1,), (1,)), ((), ())), preferred_element_type=F32
                ))
            results += [synthesis[0] + synthesis[1], synthesis[0] - synthesis[1]]
        for lb in range(nl // 8):
            items = lane_transpose([r[:, lb * 128:(lb + 1) * 128] for r in results], cycles)
            for k, item in enumerate(items):
                item = item.reshape(2, nc, chans, 128)
                item = jnp.concatenate([item[0], item[1]], axis=1)
                back[t, lb * 8 + k] = item.astype(BF16)

        to_all(back.at[t], back_in.at[t], s3_send.at[t], s3_recv.at[t])
        return carry

    lax.fori_loop(0, tans, legendre_stage, 0)

    def inverse(t):
        drain(back_in.at[t], s3_recv.at[t])
        per = 2 * chans
        unpacked[...] = back_in[t].astype(F32).reshape(unpacked.shape)
        for og in range(chans // 4):
            stack = []
            for q in range(2):
                items = [
                    unpacked[pl.ds(q * chans + og * 4 + j, everyone, stride=per), :]
                    for j in range(4)
                ]
                stack += lane_transpose(items, 2 * cycles)
            left = jnp.concatenate(stack, axis=0).T.astype(BF16)
            wave[og * 128:(og + 1) * 128, :] = jnp.dot(
                left, inverse_v[...], preferred_element_type=F32
            )

    def finish(t):
        pair = 2
        for c in range(0, chans, pair):
            part = wave[c * 2 * cycles:(c + pair) * 2 * cycles, :].reshape(pair, 2, cycles, period)
            for a in range(points // period):
                at = slice(a * period, (a + 1) * period)
                field_v[t, c:c + pair, :, :, at] = (
                    field_v[t, c:c + pair, :, :, at].astype(F32) + part
                ).astype(BF16)
            pltpu.make_async_copy(
                field_v.at[t, pl.ds(c, pair)], out_ref.at[pl.ds(c, pair), t], out_sem.at[t]
            ).start()

    inverse(0)
    u = wave[...]
    g = jax.nn.sigmoid(u)
    slope_v[...] = g * (1.0 + u * (1.0 - g))
    wave[...] = u * g
    finish(0)

    def tangent(t, carry):
        inverse(t)
        wave[...] = slope_v[...] * wave[...]
        finish(t)
        return carry

    lax.fori_loop(1, tans, tangent, 0)

    for t in range(tans):
        pltpu.make_async_copy(field_v.at[t], out_ref.at[:, t], out_sem.at[t]).wait()
    for k in range(nc - 1):
        drain(gain_own, gain_send)
    for t in range(tans):
        drain(spec.at[t, pl.ds(0, nl - 1)], s1_send.at[t])
        drain(spec.at[t, nl - 1, pl.ds(0, nc - 1)], s1_send.at[t])
        drain(back.at[t, pl.ds(0, nl - 1)], s3_send.at[t])
        drain(back.at[t, nl - 1, pl.ds(0, nc - 1)], s3_send.at[t])


def local(nl, nc, field, mix_weight, spectral_gain, legendre, slot_mode):
    chans, tans, _, cycles, points = field.shape
    slots = slot_mode.shape[0]
    degrees = spectral_gain.shape[1]
    half = degrees // 2
    step = degrees // slots
    period = points // step
    full = legendre.shape[2]
    total = chans * nc
    assert slots == 4 * nc * nl and full == nl * cycles and nl % 8 == 0
    assert 2 * cycles == 32 and chans == 8 and period == 2 * slots
    ncols = 2 * slots

    rows = chans * 2 * cycles
    small = (
        jnp.pad(spectral_gain, ((0, total + 8), (0, 0)))
        + jnp.pad(mix_weight.astype(F32), ((chans, 8), (0, degrees - total)))
        + jnp.pad(slot_mode.astype(F32)[None], ((chans + total, 7), (0, degrees - slots)))
    )
    hbm = pl.BlockSpec(memory_space=pltpu.HBM)
    dma = pltpu.SemaphoreType.DMA
    return pl.pallas_call(
        functools.partial(main_kernel, nl, nc, slots, period, step),
        out_shape=jax.ShapeDtypeStruct(field.shape, BF16),
        in_specs=[pl.BlockSpec(memory_space=pl.ANY)] + [hbm] * 2,
        out_specs=pl.BlockSpec(memory_space=pl.ANY),
        scratch_shapes=[
            pltpu.VMEM((tans, chans, 2, cycles, points), BF16),
            pltpu.VMEM((2, 4, full, half), BF16),
            pltpu.VMEM((period, ncols), BF16),
            pltpu.VMEM((ncols, period), BF16),
            pltpu.VMEM((2 * total, 2 * total), BF16),
            pltpu.VMEM((2, chans, half), F32),
            pltpu.VMEM((nc, 2, chans, half), F32),
            pltpu.VMEM((8, total, half), F32),
            pltpu.VMEM((tans, nl, nc, 16, 128), BF16),
            pltpu.VMEM((tans, nl, nc, 16, 128), BF16),
            pltpu.VMEM((full // 128, 16 * total, 128), F32),
            pltpu.VMEM((tans, nl, nc, 2 * chans, 128), BF16),
            pltpu.VMEM((tans, nl, nc, 2 * chans, 128), BF16),
            pltpu.VMEM((nl * nc * 2 * chans, 128), F32),
            pltpu.VMEM((rows, period), F32),
            pltpu.VMEM((rows, period), F32),
            pltpu.VMEM((chans + total + 8, degrees), F32),
            dma((tans,)), dma((tans,)), dma, dma, dma, dma,
            dma((tans,)), dma((tans,)), dma((tans,)), dma((tans,)),
        ],
        compiler_params=pltpu.CompilerParams(
            collective_id=0, has_side_effects=True, vmem_limit_bytes=44 * 1024 * 1024
        ),
        cost_estimate=pl.CostEstimate(
            flops=4_000_000_000, bytes_accessed=9_000_000, transcendentals=0
        ),
        name="spectral",
    )(small, field, legendre)


def solution(mesh):
    placed = (
        P("chan", None, None, "lat", None),
        P(),
        P("chan", None),
        P(None, "lat", None, None),
        P(),
    )
    return jax.shard_map(
        functools.partial(local, mesh.shape["lat"], mesh.shape["chan"]),
        mesh=mesh,
        in_specs=placed,
        out_specs=P("chan", None, None, "lat", None),
        check_vma=False,
    )
```

```python
import functools
import math

import jax
import jax.numpy as jnp
from jax import lax
from jax.experimental import pallas as pl
from jax.experimental.pallas import tpu as pltpu
from jax.sharding import PartitionSpec as P

MESH = pl.DeviceIdType.MESH
F32 = jnp.float32
BF16 = jnp.bfloat16


def lane_iota(shape, axis):
    return lax.broadcasted_iota(jnp.int32, shape, axis)


def lane_transpose(items, width):
    count = len(items)
    lane = lane_iota(items[0].shape, 1)
    items = list(items)
    bit = 1
    while bit < count:
        shift = bit * width
        upper = (lane & shift) != 0
        lanes = items[0].shape[1]
        for first in range(count):
            if first & bit:
                continue
            low, high = items[first], items[first | bit]
            items[first] = jnp.where(upper, pltpu.roll(high, shift, 1), low)
            items[first | bit] = jnp.where(upper, high, pltpu.roll(low, lanes - shift, 1))
        bit *= 2
    return items


def phase_table(modes, shifts, period, scale):
    places = lane_iota((period, modes.shape[1]), 0)
    turns = (places * modes + shifts) & (period - 1)
    quarter = jnp.abs(turns - period // 2) - period // 4
    x = quarter.astype(F32) * (2.0 * math.pi / period)
    y = x * x
    poly = 1.0 / math.factorial(13)
    for order in (11, 9, 7, 5, 3, 1):
        sign = -1.0 if (order // 2) % 2 else 1.0
        poly = poly * y + sign / math.factorial(order)
    return x * poly * scale


def bits(x, low, count):
    return lax.shift_right_logical(x, low.bit_length() - 1) & (count - 1)


def columns_of(modes, slot_of):
    slots = modes.shape[1]
    pick = (lane_iota(slot_of.shape, 0) == slot_of).astype(BF16)
    split = jnp.where(lane_iota((8, slots), 0) == 0, modes >> 4, modes & 15)
    found = jnp.dot(split.astype(F32).astype(BF16), pick, preferred_element_type=F32)
    return (found[0:1, :] * 16.0 + found[1:2, :]).astype(jnp.int32)


def main_kernel(
    nl, nc, slots, period, step,
    small_ref, field_ref, legendre_ref, out_ref,
    field_v, legendre_v, forward_v, inverse_v, mix_v, gain_own, gain_all, gain_rows,
    spec, spec_in, arranged, back, back_in, unpacked, wave, slope_v, small_v,
    field_sem, out_sem, legendre_sem, small_sem, gain_send, gain_recv,
    s1_send, s1_recv, s3_send, s3_recv,
):
    chans, tans = field_ref.shape[0], field_ref.shape[1]
    cycles, points = field_ref.shape[3], field_ref.shape[4]
    half = legendre_ref.shape[3]
    total = nc * chans
    rows = chans * 2 * cycles
    me_l, me_c = lax.axis_index("lat"), lax.axis_index("chan")
    everyone = nl * nc

    barrier = pltpu.get_barrier_semaphore()

    lats = [lax.rem(me_l + k, nl) for k in range(nl)]
    chs = [lax.rem(me_c + k, nc) for k in range(nc)]
    others = [(kl, kc) for kl in range(nl) for kc in range(nc) if kl or kc]
    others.sort(key=lambda pair: (-min(pair[0], nl - pair[0]), pair))

    def load_field(t):
        return pltpu.make_async_copy(field_ref.at[:, t], field_v.at[t], field_sem.at[t])

    load_small = pltpu.make_async_copy(small_ref, small_v, small_sem)
    load_small.start()
    load_field(0).start()
    for kl, kc in others:
        pl.semaphore_signal(
            barrier, inc=1, device_id=(lats[kl], chs[kc]), device_id_type=MESH
        )

    load_small.wait()
    mode_row = small_v[chans + total:chans + total + 1, :slots].astype(jnp.int32)
    ncols = 2 * slots
    col = lane_iota((slots, ncols), 1)
    lane = lane_iota((1, ncols), 1)
    forward_v[...] = phase_table(
        columns_of(mode_row, col >> 1), (lane & 1) * (period // 4), period,
        math.sqrt(2.0 / points),
    ).astype(BF16)

    pl.semaphore_wait(barrier, everyone - 1)

    def to_chan(source, target, send, recv):
        for other in chs[1:]:
            pltpu.make_async_remote_copy(
                src_ref=source(other), dst_ref=target, send_sem=send, recv_sem=recv,
                device_id=(me_l, other), device_id_type=MESH,
            ).start()
        pltpu.make_async_copy(source(me_c), target, recv).start()

    def to_all(source, target, span, send, recv):
        for kl, kc in others:
            pltpu.make_async_remote_copy(
                src_ref=source.at[lats[kl], chs[kc], span], dst_ref=target.at[me_l, me_c, span],
                send_sem=send, recv_sem=recv,
                device_id=(lats[kl], chs[kc]), device_id_type=MESH,
            ).start()
        pltpu.make_async_copy(
            source.at[me_l, me_c, span], target.at[me_l, me_c, span], recv
        ).start()

    groups = [(0, 1), (1, tans - 1)]
    spans = [pl.ds(first, count) for first, count in groups]

    def drain(ref, sem):
        pltpu.make_async_copy(ref, ref, sem).wait()

    def forward(t):
        total_sum = jnp.zeros((rows, forward_v.shape[1]), F32)
        for a in range(points // period):
            x = field_v[t, :, :, :, a * period:(a + 1) * period].reshape(rows, period)
            total_sum += jnp.dot(x, forward_v[...], preferred_element_type=F32)
        turned = total_sum.T.reshape(everyone, 8, rows)
        turned = jnp.concatenate([turned[:, :, :128], turned[:, :, 128:]], axis=1)
        spec[:, :, t] = turned.astype(BF16).reshape(nl, nc, 16, 128)

    load_field(0).wait()
    for t in range(1, tans):
        load_field(t).start()
    forward(0)
    to_all(spec, spec_in, spans[0], s1_send.at[0], s1_recv.at[0])
    load_legendre = pltpu.make_async_copy(
        legendre_ref.at[:, pl.ds(me_c * 4, 4)], legendre_v, legendre_sem
    )
    load_legendre.start()

    for t in range(1, tans):
        load_field(t).wait()
        forward(t)
    to_all(spec, spec_in, spans[1], s1_send.at[1], s1_recv.at[1])

    slot_of = bits(col, nc, nl) * (4 * nc) + bits(col, 1, nc) * 4 + bits(col, nl * nc, 4)
    inverse_v[...] = phase_table(
        columns_of(mode_row, slot_of), bits(lane, slots, 2) * (period // 4), period,
        math.sqrt(1.0 / slots),
    ).T.astype(BF16)

    eighth = 2 * half // 256
    x = jnp.concatenate([small_v[:chans, b * 256:(b + 1) * 256] for b in range(eighth)], axis=0)
    at_row, at_col = lane_iota((256, 256), 0), lane_iota((256, 256), 1)
    pick = (at_row == 2 * (at_col & 127) + bits(at_col, 128, 2)).astype(BF16)
    sorted_gain = jnp.zeros(x.shape, F32)
    for _ in range(3):
        term = x.astype(BF16)
        x = x - term.astype(F32)
        sorted_gain += jnp.dot(term, pick, preferred_element_type=F32)
    for b in range(eighth):
        for p in range(2):
            gain_own[p, :, b * 128:(b + 1) * 128] = (
                sorted_gain[b * chans:(b + 1) * chans, p * 128:(p + 1) * 128]
            )
    to_chan(lambda other: gain_own, gain_all.at[me_c], gain_send, gain_recv)

    weight = small_v[chans:chans + total, :total].astype(BF16)
    pick = ((lane_iota((2 * total, total), 0) & (total - 1)) == lane_iota((2 * total, total), 1))
    spread = (lane_iota((total, 2 * total), 1) >> 1 == lane_iota((total, 2 * total), 0))
    part = jnp.dot(pick.astype(BF16), weight, preferred_element_type=F32).astype(BF16)
    part = jnp.dot(part, spread.astype(BF16), preferred_element_type=F32)
    shape = (2 * total, 2 * total)
    both = (lane_iota(shape, 0) >= total) & ((lane_iota(shape, 1) & 1) == 1)
    mix_v[...] = jnp.where(both, -part, part).astype(BF16)

    load_legendre.wait()
    drain(gain_all, gain_recv)
    own_slots = 4 * nc
    degree = 2 * lane_iota((total, half), 1)
    for s in range(4):
        here = lane_iota((1, slots), 1) == me_l * own_slots + me_c * 4 + s
        mode = jnp.sum(jnp.where(here, small_v[chans + total:chans + total + 1, :slots], 0.0))
        mode = mode.astype(jnp.int32) * step
        for p in range(2):
            gain_rows[s * 2 + p] = jnp.where(
                degree + p >= mode, gain_all[:, p].reshape(total, half), 0.0
            )

    def legendre_stage(g):
        first, count = groups[g]
        drain(spec_in.at[:, :, spans[g]], s1_recv.at[g])
        mixed = []
        for t in range(first, first + count):
            x = spec_in[:, :, t].astype(F32)
            parts = []
            for lb in range(nl // 8):
                for block in range(nc):
                    for part in range(2):
                        items = [
                            x[lb * 8 + k, block, part * 8:(part + 1) * 8, :] for k in range(8)
                        ]
                        for k, item in enumerate(lane_transpose(items, cycles)):
                            row = (block * 2 + part) * 8 + k
                            arranged.at[lb][pl.ds(row, 8, stride=2 * total), :] = item
                wide = jnp.concatenate([
                    arranged[lb, j * 2 * total:(j + 1) * 2 * total, :] for j in range(8)
                ], axis=1).astype(BF16)
                parts.append(jnp.dot(mix_v[...], wide, preferred_element_type=F32).astype(BF16))
            mixed.append(parts)
        results = []
        for s in range(4):
            synthesis = []
            for p in range(2):
                pieces = []
                for parts in mixed:
                    for q in range(2):
                        at = slice((s * 2 + q) * 128, (s * 2 + q + 1) * 128)
                        cells = [m[p * total:(p + 1) * total, at] for m in parts]
                        pieces.append(
                            cells[0] if len(cells) == 1 else jnp.concatenate(cells, axis=1)
                        )
                source = jnp.concatenate(pieces, axis=0)
                table = legendre_v[p, s]
                coefficients = jnp.dot(source, table, preferred_element_type=F32)
                filtered = (
                    coefficients.reshape(2 * count, total, half) * gain_rows[s * 2 + p][None]
                ).reshape(2 * count * total, half).astype(BF16)
                synthesis.append(lax.dot_general(
                    filtered, table, (((1,), (1,)), ((), ())), preferred_element_type=F32
                ))
            results += [synthesis[0] + synthesis[1], synthesis[0] - synthesis[1]]
        for lb in range(nl // 8):
            items = lane_transpose([r[:, lb * 128:(lb + 1) * 128] for r in results], cycles)
            for k, item in enumerate(items):
                item = item.reshape(count, 2, nc, chans, 128)
                for t in range(count):
                    cell = jnp.concatenate([item[t, 0], item[t, 1]], axis=1)
                    back[lb * 8 + k, :, first + t] = cell.astype(BF16)

        to_all(back, back_in, spans[g], s3_send.at[g], s3_recv.at[g])

    for g in range(2):
        legendre_stage(g)

    def inverse(t):
        per = 2 * chans
        unpacked[...] = back_in[:, :, t].astype(F32).reshape(unpacked.shape)
        for og in range(chans // 4):
            stack = []
            for q in range(2):
                items = [
                    unpacked[pl.ds(q * chans + og * 4 + j, everyone, stride=per), :]
                    for j in range(4)
                ]
                stack += lane_transpose(items, 2 * cycles)
            left = jnp.concatenate(stack, axis=0).T.astype(BF16)
            wave[og * 128:(og + 1) * 128, :] = jnp.dot(
                left, inverse_v[...], preferred_element_type=F32
            )

    def finish(t):
        pair = 2
        for c in range(0, chans, pair):
            part = wave[c * 2 * cycles:(c + pair) * 2 * cycles, :].reshape(pair, 2, cycles, period)
            for a in range(points // period):
                at = slice(a * period, (a + 1) * period)
                field_v[t, c:c + pair, :, :, at] = (
                    field_v[t, c:c + pair, :, :, at].astype(F32) + part
                ).astype(BF16)
            pltpu.make_async_copy(
                field_v.at[t, pl.ds(c, pair)], out_ref.at[pl.ds(c, pair), t], out_sem.at[t]
            ).start()

    drain(back_in.at[:, :, spans[0]], s3_recv.at[0])
    inverse(0)
    u = wave[...]
    g = jax.nn.sigmoid(u)
    slope_v[...] = g * (1.0 + u * (1.0 - g))
    wave[...] = u * g
    finish(0)

    drain(back_in.at[:, :, spans[1]], s3_recv.at[1])
    for t in range(1, tans):
        inverse(t)
        wave[...] = slope_v[...] * wave[...]
        finish(t)

    for t in range(tans):
        pltpu.make_async_copy(field_v.at[t], out_ref.at[:, t], out_sem.at[t]).wait()
    for k in range(nc - 1):
        drain(gain_own, gain_send)
    for g, span in enumerate(spans):
        for ref, sem in ((spec, s1_send), (back, s3_send)):
            drain(ref.at[pl.ds(0, nl - 1), :, span], sem.at[g])
            drain(ref.at[nl - 1, pl.ds(0, nc - 1), span], sem.at[g])


def local(nl, nc, field, mix_weight, spectral_gain, legendre, slot_mode):
    chans, tans, _, cycles, points = field.shape
    slots = slot_mode.shape[0]
    degrees = spectral_gain.shape[1]
    half = degrees // 2
    step = degrees // slots
    period = points // step
    full = legendre.shape[2]
    total = chans * nc
    assert slots == 4 * nc * nl and full == nl * cycles and nl % 8 == 0
    assert 2 * cycles == 32 and chans == 8 and period == 2 * slots
    ncols = 2 * slots

    rows = chans * 2 * cycles
    small = (
        jnp.pad(spectral_gain, ((0, total + 8), (0, 0)))
        + jnp.pad(mix_weight.astype(F32), ((chans, 8), (0, degrees - total)))
        + jnp.pad(slot_mode.astype(F32)[None], ((chans + total, 7), (0, degrees - slots)))
    )
    hbm = pl.BlockSpec(memory_space=pltpu.HBM)
    dma = pltpu.SemaphoreType.DMA
    return pl.pallas_call(
        functools.partial(main_kernel, nl, nc, slots, period, step),
        out_shape=jax.ShapeDtypeStruct(field.shape, BF16),
        in_specs=[pl.BlockSpec(memory_space=pl.ANY)] + [hbm] * 2,
        out_specs=pl.BlockSpec(memory_space=pl.ANY),
        scratch_shapes=[
            pltpu.VMEM((tans, chans, 2, cycles, points), BF16),
            pltpu.VMEM((2, 4, full, half), BF16),
            pltpu.VMEM((period, ncols), BF16),
            pltpu.VMEM((ncols, period), BF16),
            pltpu.VMEM((2 * total, 2 * total), BF16),
            pltpu.VMEM((2, chans, half), F32),
            pltpu.VMEM((nc, 2, chans, half), F32),
            pltpu.VMEM((8, total, half), F32),
            pltpu.VMEM((nl, nc, tans, 16, 128), BF16),
            pltpu.VMEM((nl, nc, tans, 16, 128), BF16),
            pltpu.VMEM((full // 128, 16 * total, 128), F32),
            pltpu.VMEM((nl, nc, tans, 2 * chans, 128), BF16),
            pltpu.VMEM((nl, nc, tans, 2 * chans, 128), BF16),
            pltpu.VMEM((nl * nc * 2 * chans, 128), F32),
            pltpu.VMEM((rows, period), F32),
            pltpu.VMEM((rows, period), F32),
            pltpu.VMEM((chans + total + 8, degrees), F32),
            dma((tans,)), dma((tans,)), dma, dma, dma, dma,
            dma((2,)), dma((2,)), dma((2,)), dma((2,)),
        ],
        compiler_params=pltpu.CompilerParams(
            collective_id=0, has_side_effects=True, vmem_limit_bytes=44 * 1024 * 1024
        ),
        cost_estimate=pl.CostEstimate(
            flops=4_000_000_000, bytes_accessed=9_000_000, transcendentals=0
        ),
        name="spectral",
    )(small, field, legendre)


def solution(mesh):
    placed = (
        P("chan", None, None, "lat", None),
        P(),
        P("chan", None),
        P(None, "lat", None, None),
        P(),
    )
    return jax.shard_map(
        functools.partial(local, mesh.shape["lat"], mesh.shape["chan"]),
        mesh=mesh,
        in_specs=placed,
        out_specs=P("chan", None, None, "lat", None),
        check_vma=False,
    )
```

```python
import functools
import math

import jax
import jax.numpy as jnp
from jax import lax
from jax.experimental import pallas as pl
from jax.experimental.pallas import tpu as pltpu
from jax.sharding import PartitionSpec as P

MESH = pl.DeviceIdType.MESH
F32 = jnp.float32
BF16 = jnp.bfloat16


def lane_iota(shape, axis):
    return lax.broadcasted_iota(jnp.int32, shape, axis)


def lane_transpose(items, width):
    count = len(items)
    lane = lane_iota(items[0].shape, 1)
    items = list(items)
    bit = 1
    while bit < count:
        shift = bit * width
        upper = (lane & shift) != 0
        lanes = items[0].shape[1]
        for first in range(count):
            if first & bit:
                continue
            low, high = items[first], items[first | bit]
            items[first] = jnp.where(upper, pltpu.roll(high, shift, 1), low)
            items[first | bit] = jnp.where(upper, high, pltpu.roll(low, lanes - shift, 1))
        bit *= 2
    return items


def phase_table(modes, shifts, period, scale):
    places = lane_iota((period, modes.shape[1]), 0)
    turns = (places * modes + shifts) & (period - 1)
    quarter = jnp.abs(turns - period // 2) - period // 4
    x = quarter.astype(F32) * (2.0 * math.pi / period)
    y = x * x
    poly = 1.0 / math.factorial(13)
    for order in (11, 9, 7, 5, 3, 1):
        sign = -1.0 if (order // 2) % 2 else 1.0
        poly = poly * y + sign / math.factorial(order)
    return x * poly * scale


def bits(x, low, count):
    return lax.shift_right_logical(x, low.bit_length() - 1) & (count - 1)


def columns_of(modes, slot_of):
    slots = modes.shape[1]
    pick = (lane_iota(slot_of.shape, 0) == slot_of).astype(BF16)
    split = jnp.where(lane_iota((8, slots), 0) == 0, modes >> 4, modes & 15)
    found = jnp.dot(split.astype(F32).astype(BF16), pick, preferred_element_type=F32)
    return (found[0:1, :] * 16.0 + found[1:2, :]).astype(jnp.int32)


def main_kernel(
    nl, nc, slots, period, step,
    small_ref, field_ref, legendre_ref, out_ref,
    field_v, legendre_v, forward_v, inverse_v, mix_v, gain_own, gain_all, gain_rows,
    spec, spec_in, arranged, back, back_in, unpacked, wave, slope_v, small_v,
    field_sem, out_sem, legendre_sem, small_sem, gain_send, gain_recv,
    s1_send, s1_recv, s3_send, s3_recv,
):
    chans, tans = field_ref.shape[0], field_ref.shape[1]
    cycles, points = field_ref.shape[3], field_ref.shape[4]
    half = legendre_ref.shape[3]
    total = nc * chans
    rows = chans * 2 * cycles
    me_l, me_c = lax.axis_index("lat"), lax.axis_index("chan")
    everyone = nl * nc

    barrier = pltpu.get_barrier_semaphore()

    lats = [lax.rem(me_l + k, nl) for k in range(nl)]
    chs = [lax.rem(me_c + k, nc) for k in range(nc)]
    others = [(kl, kc) for kl in range(nl) for kc in range(nc) if kl or kc]
    others.sort(key=lambda pair: (-min(pair[0], nl - pair[0]), pair))
    half_way = (len(others) + 1) // 2
    others = [
        pair for k in range(half_way)
        for pair in dict.fromkeys((others[k], others[len(others) - 1 - k]))
    ]

    def load_field(t):
        return pltpu.make_async_copy(field_ref.at[:, t], field_v.at[t], field_sem.at[t])

    load_small = pltpu.make_async_copy(small_ref, small_v, small_sem)
    load_small.start()
    load_field(0).start()
    for kl, kc in others:
        pl.semaphore_signal(
            barrier, inc=1, device_id=(lats[kl], chs[kc]), device_id_type=MESH
        )

    load_small.wait()
    mode_row = small_v[chans + total:chans + total + 1, :slots].astype(jnp.int32)
    ncols = 2 * slots
    col = lane_iota((slots, ncols), 1)
    lane = lane_iota((1, ncols), 1)
    forward_v[...] = phase_table(
        columns_of(mode_row, col >> 1), (lane & 1) * (period // 4), period,
        math.sqrt(2.0 / points),
    ).astype(BF16)

    pl.semaphore_wait(barrier, everyone - 1)

    def to_chan(source, target, send, recv):
        for other in chs[1:]:
            pltpu.make_async_remote_copy(
                src_ref=source(other), dst_ref=target, send_sem=send, recv_sem=recv,
                device_id=(me_l, other), device_id_type=MESH,
            ).start()
        pltpu.make_async_copy(source(me_c), target, recv).start()

    def to_all(source, target, send, recv):
        for kl, kc in others:
            pltpu.make_async_remote_copy(
                src_ref=source.at[lats[kl], chs[kc]], dst_ref=target.at[me_l, me_c],
                send_sem=send, recv_sem=recv,
                device_id=(lats[kl], chs[kc]), device_id_type=MESH,
            ).start()
        pltpu.make_async_copy(source.at[me_l, me_c], target.at[me_l, me_c], recv).start()

    def drain(ref, sem):
        pltpu.make_async_copy(ref, ref, sem).wait()

    def forward(t):
        total_sum = jnp.zeros((rows, forward_v.shape[1]), F32)
        for a in range(points // period):
            x = field_v[t, :, :, :, a * period:(a + 1) * period].reshape(rows, period)
            total_sum += jnp.dot(x, forward_v[...], preferred_element_type=F32)
        turned = total_sum.T.reshape(everyone, 8, rows)
        turned = jnp.concatenate([turned[:, :, :128], turned[:, :, 128:]], axis=1)
        spec[t] = turned.astype(BF16).reshape(spec.shape[1:])
        to_all(spec.at[t], spec_in.at[t], s1_send.at[t], s1_recv.at[t])

    load_field(0).wait()
    for t in range(1, tans):
        load_field(t).start()
    forward(0)
    load_legendre = pltpu.make_async_copy(
        legendre_ref.at[:, pl.ds(me_c * 4, 4)], legendre_v, legendre_sem
    )
    load_legendre.start()

    def forward_next(t, carry):
        pltpu.make_async_copy(field_ref.at[:, t], field_v.at[t], field_sem.at[t]).wait()
        forward(t)
        return carry

    lax.fori_loop(1, tans, forward_next, 0)

    slot_of = bits(col, nc, nl) * (4 * nc) + bits(col, 1, nc) * 4 + bits(col, nl * nc, 4)
    inverse_v[...] = phase_table(
        columns_of(mode_row, slot_of), bits(lane, slots, 2) * (period // 4), period,
        math.sqrt(1.0 / slots),
    ).T.astype(BF16)

    eighth = 2 * half // 256
    x = jnp.concatenate([small_v[:chans, b * 256:(b + 1) * 256] for b in range(eighth)], axis=0)
    at_row, at_col = lane_iota((256, 256), 0), lane_iota((256, 256), 1)
    pick = (at_row == 2 * (at_col & 127) + bits(at_col, 128, 2)).astype(BF16)
    sorted_gain = jnp.zeros(x.shape, F32)
    for _ in range(3):
        term = x.astype(BF16)
        x = x - term.astype(F32)
        sorted_gain += jnp.dot(term, pick, preferred_element_type=F32)
    for b in range(eighth):
        for p in range(2):
            gain_own[p, :, b * 128:(b + 1) * 128] = (
                sorted_gain[b * chans:(b + 1) * chans, p * 128:(p + 1) * 128]
            )
    to_chan(lambda other: gain_own, gain_all.at[me_c], gain_send, gain_recv)

    weight = small_v[chans:chans + total, :total].astype(BF16)
    pick = ((lane_iota((2 * total, total), 0) & (total - 1)) == lane_iota((2 * total, total), 1))
    spread = (lane_iota((total, 2 * total), 1) >> 1 == lane_iota((total, 2 * total), 0))
    part = jnp.dot(pick.astype(BF16), weight, preferred_element_type=F32).astype(BF16)
    part = jnp.dot(part, spread.astype(BF16), preferred_element_type=F32)
    shape = (2 * total, 2 * total)
    both = (lane_iota(shape, 0) >= total) & ((lane_iota(shape, 1) & 1) == 1)
    mix_v[...] = jnp.where(both, -part, part).astype(BF16)

    load_legendre.wait()
    drain(gain_all, gain_recv)
    own_slots = 4 * nc
    degree = 2 * lane_iota((total, half), 1)
    for s in range(4):
        here = lane_iota((1, slots), 1) == me_l * own_slots + me_c * 4 + s
        mode = jnp.sum(jnp.where(here, small_v[chans + total:chans + total + 1, :slots], 0.0))
        mode = mode.astype(jnp.int32) * step
        for p in range(2):
            gain_rows[s * 2 + p] = jnp.where(
                degree + p >= mode, gain_all[:, p].reshape(total, half), 0.0
            )

    def legendre_stage(t, carry):
        drain(spec_in.at[t], s1_recv.at[t])
        x = spec_in[t].astype(F32)
        mixed = []
        for lb in range(nl // 8):
            for block in range(nc):
                for part in range(2):
                    items = [
                        x[lb * 8 + k, block, part * 8:(part + 1) * 8, :] for k in range(8)
                    ]
                    for k, item in enumerate(lane_transpose(items, cycles)):
                        row = (block * 2 + part) * 8 + k
                        arranged.at[lb][pl.ds(row, 8, stride=2 * total), :] = item
            wide = jnp.concatenate([
                arranged[lb, j * 2 * total:(j + 1) * 2 * total, :] for j in range(8)
            ], axis=1).astype(BF16)
            mixed.append(jnp.dot(mix_v[...], wide, preferred_element_type=F32).astype(BF16))
        results = []
        for s in range(4):
            synthesis = []
            for p in range(2):
                source = jnp.concatenate([
                    jnp.concatenate([
                        m[p * total:(p + 1) * total, (s * 2 + q) * 128:(s * 2 + q + 1) * 128]
                        for m in mixed
                    ], axis=1) if len(mixed) > 1 else
                    mixed[0][p * total:(p + 1) * total, (s * 2 + q) * 128:(s * 2 + q + 1) * 128]
                    for q in range(2)
                ], axis=0)
                table = legendre_v[p, s]
                coefficients = jnp.dot(source, table, preferred_element_type=F32)
                filtered = (
                    coefficients.reshape(2, total, half) * gain_rows[s * 2 + p][None]
                ).reshape(2 * total, half).astype(BF16)
                synthesis.append(lax.dot_general(
                    filtered, table, (((1,), (1,)), ((), ())), preferred_element_type=F32
                ))
            results += [synthesis[0] + synthesis[1], synthesis[0] - synthesis[1]]
        for lb in range(nl // 8):
            items = lane_transpose([r[:, lb * 128:(lb + 1) * 128] for r in results], cycles)
            for k, item in enumerate(items):
                item = item.reshape(2, nc, chans, 128)
                item = jnp.concatenate([item[0], item[1]], axis=1)
                back[t, lb * 8 + k] = item.astype(BF16)

        to_all(back.at[t], back_in.at[t], s3_send.at[t], s3_recv.at[t])
        return carry

    lax.fori_loop(0, tans, legendre_stage, 0)

    def inverse(t):
        drain(back_in.at[t], s3_recv.at[t])
        per = 2 * chans
        unpacked[...] = back_in[t].astype(F32).reshape(unpacked.shape)
        for og in range(chans // 4):
            stack = []
            for q in range(2):
                items = [
                    unpacked[pl.ds(q * chans + og * 4 + j, everyone, stride=per), :]
                    for j in range(4)
                ]
                stack += lane_transpose(items, 2 * cycles)
            left = jnp.concatenate(stack, axis=0).T.astype(BF16)
            wave[og * 128:(og + 1) * 128, :] = jnp.dot(
                left, inverse_v[...], preferred_element_type=F32
            )

    def finish(t):
        pair = 2
        for c in range(0, chans, pair):
            part = wave[c * 2 * cycles:(c + pair) * 2 * cycles, :].reshape(pair, 2, cycles, period)
            for a in range(points // period):
                at = slice(a * period, (a + 1) * period)
                field_v[t, c:c + pair, :, :, at] = (
                    field_v[t, c:c + pair, :, :, at].astype(F32) + part
                ).astype(BF16)
            pltpu.make_async_copy(
                field_v.at[t, pl.ds(c, pair)], out_ref.at[pl.ds(c, pair), t], out_sem.at[t]
            ).start()

    inverse(0)
    u = wave[...]
    g = jax.nn.sigmoid(u)
    slope_v[...] = g * (1.0 + u * (1.0 - g))
    wave[...] = u * g
    finish(0)

    def tangent(t, carry):
        inverse(t)
        wave[...] = slope_v[...] * wave[...]
        finish(t)
        return carry

    lax.fori_loop(1, tans, tangent, 0)

    for t in range(tans):
        pltpu.make_async_copy(field_v.at[t], out_ref.at[:, t], out_sem.at[t]).wait()
    for k in range(nc - 1):
        drain(gain_own, gain_send)
    for t in range(tans):
        drain(spec.at[t, pl.ds(0, nl - 1)], s1_send.at[t])
        drain(spec.at[t, nl - 1, pl.ds(0, nc - 1)], s1_send.at[t])
        drain(back.at[t, pl.ds(0, nl - 1)], s3_send.at[t])
        drain(back.at[t, nl - 1, pl.ds(0, nc - 1)], s3_send.at[t])


def local(nl, nc, field, mix_weight, spectral_gain, legendre, slot_mode):
    chans, tans, _, cycles, points = field.shape
    slots = slot_mode.shape[0]
    degrees = spectral_gain.shape[1]
    half = degrees // 2
    step = degrees // slots
    period = points // step
    full = legendre.shape[2]
    total = chans * nc
    assert slots == 4 * nc * nl and full == nl * cycles and nl % 8 == 0
    assert 2 * cycles == 32 and chans == 8 and period == 2 * slots
    ncols = 2 * slots

    rows = chans * 2 * cycles
    small = (
        jnp.pad(spectral_gain, ((0, total + 8), (0, 0)))
        + jnp.pad(mix_weight.astype(F32), ((chans, 8), (0, degrees - total)))
        + jnp.pad(slot_mode.astype(F32)[None], ((chans + total, 7), (0, degrees - slots)))
    )
    hbm = pl.BlockSpec(memory_space=pltpu.HBM)
    dma = pltpu.SemaphoreType.DMA
    return pl.pallas_call(
        functools.partial(main_kernel, nl, nc, slots, period, step),
        out_shape=jax.ShapeDtypeStruct(field.shape, BF16),
        in_specs=[pl.BlockSpec(memory_space=pl.ANY)] + [hbm] * 2,
        out_specs=pl.BlockSpec(memory_space=pl.ANY),
        scratch_shapes=[
            pltpu.VMEM((tans, chans, 2, cycles, points), BF16),
            pltpu.VMEM((2, 4, full, half), BF16),
            pltpu.VMEM((period, ncols), BF16),
            pltpu.VMEM((ncols, period), BF16),
            pltpu.VMEM((2 * total, 2 * total), BF16),
            pltpu.VMEM((2, chans, half), F32),
            pltpu.VMEM((nc, 2, chans, half), F32),
            pltpu.VMEM((8, total, half), F32),
            pltpu.VMEM((tans, nl, nc, 16, 128), BF16),
            pltpu.VMEM((tans, nl, nc, 16, 128), BF16),
            pltpu.VMEM((full // 128, 16 * total, 128), F32),
            pltpu.VMEM((tans, nl, nc, 2 * chans, 128), BF16),
            pltpu.VMEM((tans, nl, nc, 2 * chans, 128), BF16),
            pltpu.VMEM((nl * nc * 2 * chans, 128), F32),
            pltpu.VMEM((rows, period), F32),
            pltpu.VMEM((rows, period), F32),
            pltpu.VMEM((chans + total + 8, degrees), F32),
            dma((tans,)), dma((tans,)), dma, dma, dma, dma,
            dma((tans,)), dma((tans,)), dma((tans,)), dma((tans,)),
        ],
        compiler_params=pltpu.CompilerParams(
            collective_id=0, has_side_effects=True, vmem_limit_bytes=44 * 1024 * 1024
        ),
        cost_estimate=pl.CostEstimate(
            flops=4_000_000_000, bytes_accessed=9_000_000, transcendentals=0
        ),
        name="spectral",
    )(small, field, legendre)


def solution(mesh):
    placed = (
        P("chan", None, None, "lat", None),
        P(),
        P("chan", None),
        P(None, "lat", None, None),
        P(),
    )
    return jax.shard_map(
        functools.partial(local, mesh.shape["lat"], mesh.shape["chan"]),
        mesh=mesh,
        in_specs=placed,
        out_specs=P("chan", None, None, "lat", None),
        check_vma=False,
    )
```
